32 devices in a mesh: expert: 16 (over z, y, x), fsdp: 2 (over core).
Axes of the slice: x: 2, y: 2, z: 4, core: 2. Of those that a mesh axis runs over, the one named last changes fastest.
Arguments:
- hidden_in: bfloat16 [8192, 2048], P(('expert', 'fsdp')), may hold values from -6 to 6
- prenorm_gain: bfloat16 [2048], P(('expert', 'fsdp')), may hold values from 0.099609375 to 1.8984375
- query_weight: bfloat16 [2048, 2048], P(('expert', 'fsdp')), may hold values from -0.125 to 0.125
- key_weight: bfloat16 [2048, 2048], P(('expert', 'fsdp')), may hold values from -0.125 to 0.125
- value_weight: bfloat16 [2048, 2048], P(('expert', 'fsdp')), may hold values from -0.125 to 0.125
- querynorm_gain: bfloat16 [128], P(('expert', 'fsdp')), may hold values from 0.099609375 to 1.8984375
- keynorm_gain: bfloat16 [128], P(('expert', 'fsdp')), may hold values from 0.099609375 to 1.8984375
- output_weight: bfloat16 [2048, 2048], P(('expert', 'fsdp')), may hold values from -2 to 2
- postnorm_gain: bfloat16 [2048], P(('expert', 'fsdp')), may hold values from 0.099609375 to 1.8984375
- router_weight: bfloat16 [2048, 16], P(('expert', 'fsdp')), may hold values from -0.0625 to 0.0625
- expert_inner: bfloat16 [16, 2048, 2048], P('expert', 'fsdp'), may hold values from -0.125 to 0.125
- expert_outer: bfloat16 [16, 1024, 2048], P('expert', 'fsdp'), may hold values from -0.75 to 0.75
- expert_ids: int32 [8192, 8], P(('expert', 'fsdp')), may hold values from 0 to 15, all different within a row
- pair_order: int32 [32, 2048], P(('expert', 'fsdp')), may hold values from 0 to 2047, each once within a row
- sequence_lengths: int32 [8], replicated, may hold values from 256 to 1024, as said below
- cotangent: bfloat16 [8192, 2048], P(('expert', 'fsdp')), may hold values from -6 to 6
Outputs:
- layer_out: bfloat16 [8192, 2048], P(('expert', 'fsdp'))
- input_grad: float32 [8192, 2048], P(('expert', 'fsdp'))
- prenorm_grad: float32 [2048], P(('expert', 'fsdp'))
- query_grad: float32 [2048, 2048], P(('expert', 'fsdp'))
- key_grad: float32 [2048, 2048], P(('expert', 'fsdp'))
- value_grad: float32 [2048, 2048], P(('expert', 'fsdp'))
- querynorm_grad: float32 [128], P(('expert', 'fsdp'))
- keynorm_grad: float32 [128], P(('expert', 'fsdp'))
- output_grad: float32 [2048, 2048], P(('expert', 'fsdp'))
- postnorm_grad: float32 [2048], P(('expert', 'fsdp'))
- router_grad: float32 [2048, 16], P(('expert', 'fsdp'))
- inner_grad: float32 [16, 2048, 2048], P('expert', 'fsdp')
- outer_grad: float32 [16, 1024, 2048], P('expert', 'fsdp')
The draws below stay inside these ranges and needn't reach their ends.
Inputs may be any that keep to these rules, and one draw needn't show every extreme that they name: `sequence_lengths`: a sequence's live tokens fill the start of its 1024 places; some sequence is 1024 long and some 1024 // 4. `expert_ids`: each row names 8 different experts. `pair_order`: each row is a permutation.
All inputs are finite; a program needn't handle non-finite values.
Results may differ from the reference program's by a relative error of at most 0.02.
Values may be sent and summed in bfloat16 or wider, within the bound.
No kernel may reach another device: no remote copies, remote signals or barrier semaphores. Data moves between devices by JAX's collectives and lax.ppermute only.
A program may use at most 320 MiB of HBM per device.

```python
import math
import jax
import jax.numpy as jnp
from jax import lax

D = 2048
HEADS = 16
HEAD = 128
EFF = 1024
TOPK = 8
TOK_DEV = 256
EXPERTS = 16
SLOT = 1024
TOKENS = 8192
SEQS = 8
CAP = 128
N_EXPERT = 16
N_FSDP = 2


def draw_sequence_lengths(key, part):
    key = jax.random.fold_in(key, 7)
    seq_count = TOKENS // SLOT
    key_lengths, key_pick = jax.random.split(key)
    drawn_lengths = jax.random.randint(key_lengths, (seq_count,), SLOT // 4, SLOT + 1)
    longest = jax.random.randint(key_pick, (), 0, seq_count)
    shortest = (longest + 1) % seq_count
    positions = jnp.arange(seq_count)
    drawn_lengths = jnp.where(positions == longest, SLOT, drawn_lengths)
    drawn_lengths = jnp.where(positions == shortest, SLOT // 4, drawn_lengths)
    return drawn_lengths.astype(jnp.int32)


def shard_levels(stream_key, shape, cuts, low, largest):
    level = 1.0
    for axis_at, parts in cuts:
        steps = jax.random.uniform(jax.random.fold_in(jax.random.fold_in(stream_key, 6), axis_at), (parts,), jnp.float32, low / len(cuts), largest / len(cuts))
        level = level * jnp.repeat(jnp.exp(steps), shape[axis_at] // parts).reshape((-1,) + (1,) * (len(shape) - 1 - axis_at))
    return level


def choose_distinct(own_key, rows, count, top, lift):
    order = jax.random.permutation(jax.random.fold_in(own_key, 1), count)
    boost = order
    for power in range(3):
        boost = boost * boost // count
    boost = boost * lift // count
    chance = jax.random.randint(jax.random.fold_in(own_key, 2), (rows, count), 0, 4096) + boost
    sure = jax.random.permutation(jax.random.fold_in(own_key, 3), rows)[jnp.arange(count) % rows]
    chance = jnp.where(jnp.arange(rows)[:, None] == sure[None, :], 1 << 14, chance)
    merit = chance * count + jnp.arange(count)
    return lax.top_k(merit.astype(jnp.int32), top)[1].astype(jnp.int32)


def scatter_about(key, dims, width, reach, pieces=(), held_as=jnp.bfloat16):
    loudness = shard_levels(key, dims, pieces, -0.22, 0.18) if pieces else 1.0
    drawn = jax.random.normal(key, dims, jnp.float32) * width * loudness
    return jnp.minimum(jnp.maximum(drawn, -reach), reach).astype(held_as)


def setup_inputs(seed: int = 0) -> dict:
    key_list = jax.random.split(jax.random.key(seed), 17)
    return {
        "hidden_in": scatter_about(key_list[0], (TOKENS, D), 1.0, 6.0, ((0, 32),)),
        "prenorm_gain": jnp.clip(1.0 + 0.18 * jax.random.normal(key_list[1], (D,), jnp.float32), 0.099609375, 1.8984375).astype(jnp.bfloat16),
        "query_weight": scatter_about(key_list[2], (D, D), D ** -0.5, 0.125, ((0, 32),)),
        "key_weight": scatter_about(key_list[3], (D, D), D ** -0.5, 0.125, ((0, 32),)),
        "value_weight": scatter_about(key_list[4], (D, D), D ** -0.5, 0.125, ((0, 32),)),
        "querynorm_gain": jnp.clip(1.0 + 0.18 * jax.random.normal(key_list[5], (HEAD,), jnp.float32), 0.099609375, 1.8984375).astype(jnp.bfloat16),
        "keynorm_gain": jnp.clip(1.0 + 0.18 * jax.random.normal(key_list[6], (HEAD,), jnp.float32), 0.099609375, 1.8984375).astype(jnp.bfloat16),
        "output_weight": scatter_about(key_list[7], (D, D), (max(D // 256, 1)) ** -0.5, 2.0, ((0, 32),)),
        "postnorm_gain": jnp.clip(1.0 + 0.18 * jax.random.normal(key_list[8], (D,), jnp.float32), 0.099609375, 1.8984375).astype(jnp.bfloat16),
        "router_weight": scatter_about(key_list[9], (D, EXPERTS), (4 * D) ** -0.5, 0.0625, ((0, 32),)),
        "expert_inner": scatter_about(key_list[10], (EXPERTS, D, 2 * EFF), D ** -0.5, 0.125, ((0, 16), (1, 2))),
        "expert_outer": scatter_about(key_list[11], (EXPERTS, EFF, D), (max(EFF // 16, 1)) ** -0.5, 0.75, ((0, 16), (1, 2))),
        "expert_ids": choose_distinct(key_list[12], TOKENS, EXPERTS, TOPK, 4096),
        "pair_order": jax.vmap(lambda own: jax.random.permutation(own, TOK_DEV * TOPK))(jax.random.split(key_list[13], (N_EXPERT * N_FSDP))).reshape((N_EXPERT * N_FSDP, TOK_DEV * TOPK)).astype(jnp.int32),
        "sequence_lengths": draw_sequence_lengths(jax.random.fold_in(key_list[16], 71), 0),
        "cotangent": scatter_about(key_list[15], (TOKENS, D), 1.0, 6.0, ((0, 32),)),
    }


epsilon = 1e-06
rope_base = 10000.0
masked = -1e+30
precise = lax.Precision.HIGHEST

@jax.custom_vjp
def low(v):
    return lax.optimization_barrier(v.astype(jnp.bfloat16)).astype(jnp.float32)

@jax.custom_vjp
def low_back(v):
    return v

def low_keep(v):
    return (low(v), None)

def low_pass(kept, grad):
    return (grad,)

def back_keep(v):
    return (v, None)

def back_low(kept, grad):
    return (low(grad),)
low.defvjp(low_keep, low_pass)
low_back.defvjp(back_keep, back_low)

def matmul(left, right):
    return jnp.dot(left, right, precision=precise, preferred_element_type=jnp.float32)

def rms_scale(values, gain):
    inverse = lax.rsqrt(lax.optimization_barrier(jnp.mean(values * values, axis=-1, keepdims=True)) + epsilon)
    return values * inverse * gain

def rotary_tables(positions):
    half_width = HEAD // 2
    freq_steps = jnp.arange(half_width).astype(jnp.float32)
    frequency = jnp.exp(freq_steps * (-2.0 * math.log(rope_base) / HEAD))
    angles = positions.astype(jnp.float32)[:, None] * frequency[None, :]
    return (jnp.cos(angles)[:, None, :], jnp.sin(angles)[:, None, :])

def rotate(values, cosine_table, sine_table):
    half_width = HEAD // 2
    lower_half = values[..., :half_width]
    upper_half = values[..., half_width:]
    return jnp.concatenate([lower_half * cosine_table - upper_half * sine_table, upper_half * cosine_table + lower_half * sine_table], axis=-1)

def attend(block_data):
    queries, key_rows, value_rows, length = block_data
    scores = jnp.einsum('qhd,khd->hqk', queries, key_rows, precision=precise) * (1.0 / math.sqrt(HEAD))
    scores = low_back(scores)
    key_live = jnp.arange(SLOT) < length
    scores = jnp.where(key_live[None, None, :], scores, masked)
    peak_score = lax.optimization_barrier(jnp.max(scores, axis=-1, keepdims=True))
    exponent = jnp.exp(scores - peak_score)
    attention = exponent / lax.optimization_barrier(jnp.sum(exponent, axis=-1, keepdims=True))
    return jnp.einsum('hqk,khd->qhd', low(attention), value_rows, precision=precise)

def block_ranks(block_data):
    pair_expert, pair_key, pair_live = block_data
    earlier = (pair_expert[None, :] == pair_expert[:, None]) & (pair_key[None, :] < pair_key[:, None]) & pair_live[None, :]
    return lax.optimization_barrier(jnp.sum(earlier.astype(jnp.int32), axis=1))

def reference(hidden_in, prenorm_gain, query_weight, key_weight, value_weight, querynorm_gain, keynorm_gain, output_weight, postnorm_gain, router_weight, expert_inner, expert_outer, expert_ids, pair_order, sequence_lengths, cotangent):
    block_count = N_EXPERT * N_FSDP
    token_index = jnp.arange(TOKENS, dtype=jnp.int32)
    positions = token_index % SLOT
    token_live = positions < sequence_lengths[token_index // SLOT]
    token_block = token_index // TOK_DEV
    pair_live = jnp.repeat(token_live, TOPK).reshape(block_count, TOK_DEV * TOPK)
    pair_rank = lax.map(block_ranks, (expert_ids.reshape(block_count, TOK_DEV * TOPK), pair_order, pair_live)).reshape(TOKENS, TOPK)
    kept_pair = token_live[:, None] & (pair_rank < CAP)
    cosine_table, sine_table = rotary_tables(positions)
    route_hot = (expert_ids[:, :, None] == jnp.arange(EXPERTS, dtype=jnp.int32)[None, None, :]).astype(jnp.float32)
    row_total = block_count * CAP
    shaped = (SEQS, SLOT, HEADS, HEAD)

    def forward(hidden, first_gain, query_proj, key_proj, value_proj, query_scale, key_scale, output_proj, second_gain, router, inner_weight, outer_weight):
        normed = low(rms_scale(hidden, first_gain))
        query_raw = low_back(matmul(normed, query_proj)).reshape(TOKENS, HEADS, HEAD)
        key_raw = low_back(matmul(normed, key_proj)).reshape(TOKENS, HEADS, HEAD)
        value_rows = low_back(low(matmul(normed, value_proj))).reshape(TOKENS, HEADS, HEAD)
        queries = low(rotate(rms_scale(query_raw, query_scale), cosine_table, sine_table))
        key_rows = low(rotate(rms_scale(key_raw, key_scale), cosine_table, sine_table))
        attended = lax.map(jax.checkpoint(attend), (queries.reshape(shaped), key_rows.reshape(shaped), value_rows.reshape(shaped), sequence_lengths))
        attended = low_back(low(attended.reshape(TOKENS, D)))
        branch = low_back(matmul(attended, output_proj))
        residual = hidden + branch
        mixed_in = low(rms_scale(residual, second_gain))
        logits = low_back(matmul(mixed_in, router))
        chosen = lax.optimization_barrier(jnp.sum(route_hot * logits[:, None, :], axis=-1))
        gate_soft = jax.nn.softmax(chosen, axis=-1)

        def expert_step(running, expert):
            chosen_pair = (expert_ids == expert) & kept_pair
            routed = jnp.any(chosen_pair, axis=1)
            rank_of = lax.optimization_barrier(jnp.sum(jnp.where(chosen_pair, pair_rank, 0), axis=1))
            gate_share = lax.optimization_barrier(jnp.sum(jnp.where(chosen_pair, gate_soft, 0.0), axis=1))
            row_index = jnp.where(routed, token_block * CAP + rank_of, row_total).astype(jnp.int32)
            row_inputs = jnp.zeros((row_total + 1, D), jnp.float32).at[row_index].add(mixed_in)[:row_total]
            row_inputs = low_back(row_inputs)
            inner_now = lax.dynamic_index_in_dim(inner_weight, expert, 0, keepdims=False)
            outer_now = lax.dynamic_index_in_dim(outer_weight, expert, 0, keepdims=False)
            gate_up = low_back(matmul(row_inputs, inner_now))
            hidden_rows = low(jax.nn.silu(gate_up[:, :EFF]) * gate_up[:, EFF:])
            result = low_back(low(matmul(hidden_rows, outer_now)))
            result = jnp.concatenate([result, jnp.zeros((1, D), jnp.float32)], axis=0)
            return (running + gate_share[:, None] * result[row_index], None)
        mixed, unused = lax.scan(jax.checkpoint(expert_step), jnp.zeros((TOKENS, D), jnp.float32), jnp.arange(EXPERTS, dtype=jnp.int32))
        return residual + mixed
    floats = tuple((array.astype(jnp.float32) for array in (hidden_in, prenorm_gain, query_weight, key_weight, value_weight, querynorm_gain, keynorm_gain, output_weight, postnorm_gain, router_weight, expert_inner, expert_outer)))
    result, pullback = jax.vjp(forward, *floats)
    grads = pullback(cotangent.astype(jnp.float32) * token_live[:, None].astype(jnp.float32))
    return (result.astype(jnp.bfloat16), grads[0], grads[1], grads[2], grads[3], grads[4], grads[5], grads[6], grads[7], grads[8], grads[9], grads[10], grads[11])
```

```python
import math

import jax
import jax.numpy as jnp
from jax import lax
from jax.experimental import pallas as pl
from jax.experimental.pallas import tpu as pltpu
from jax.sharding import PartitionSpec as P

HEAD = 128
EFF = 1024
TOPK = 8
PLANES = 4

epsilon = 1e-06
rope_base = 10000.0
masked = -1e30
bf16 = jnp.bfloat16
f32 = jnp.float32
score_scale = 1.0 / math.sqrt(HEAD)
VMEM_BYTES = 40 * 1024 * 1024


def swap(block, axis, mask):
    count = lax.axis_size(axis)
    return lax.ppermute(block, axis, [(i, i ^ mask) for i in range(count)])


def contract_rows(left, right, out=f32):
    return lax.dot_general(
        left, right, (((0,), (0,)), ((), ())), preferred_element_type=f32
    ).astype(out)


def contract_cols(left, right, out=f32):
    return lax.dot_general(
        left, right, (((1,), (1,)), ((), ())), preferred_element_type=f32
    ).astype(out)


def matmul(left, right):
    return jnp.dot(left, right, preferred_element_type=f32)


def rms_scale(values, gain):
    inverse = lax.rsqrt(jnp.mean(values * values, axis=-1, keepdims=True) + epsilon)
    return (values * inverse * gain, inverse)


def rms_back(values, inverse, gain, upstream):
    scaled = upstream * gain
    inner_sum = jnp.sum(scaled * values, axis=-1, keepdims=True)
    length_now = values.shape[-1]
    grad_values = inverse * scaled - values * (inverse * inverse * inverse) * (
        inner_sum / length_now
    )
    return (grad_values, upstream * values * inverse)


def rotary_tables(positions):
    half_width = HEAD // 2
    freq_steps = jnp.arange(half_width, dtype=f32)
    frequency = jnp.exp(freq_steps * (-2.0 * math.log(rope_base) / HEAD))
    angles = positions.astype(f32)[:, None] * frequency[None, :]
    cosine, sine = jnp.cos(angles), jnp.sin(angles)
    return jnp.stack(
        [
            jnp.concatenate([cosine, cosine], axis=-1),
            jnp.concatenate([-sine, sine], axis=-1),
        ]
    )


def unrope(upstream, cosine, sine):
    return upstream * cosine - pltpu.roll(upstream, HEAD // 2, 1) * sine


def normed_rope(values, gain, cosine, sine):
    normed, inverse = rms_scale(values, gain)
    turned = normed * cosine + pltpu.roll(normed, HEAD // 2, 1) * sine
    return turned.astype(bf16), inverse, normed


def attention_forward(query_raw, key_raw, value_low, tables, scales, live):
    queries, half = query_raw.shape
    span = key_raw.shape[0]
    heads = half // HEAD
    step = queries // 2

    def kernel(q_ref, k_ref, v_ref, table_ref, scale_ref, live_ref, out_ref, lse_ref):
        cosine, sine = table_ref[0], table_ref[1]
        key_low, _, _ = normed_rope(k_ref[...], scale_ref[1:2], cosine, sine)
        value_turned = v_ref[...].astype(f32).T.astype(bf16)
        live_now = jnp.concatenate([live_ref[...]] * (step // HEAD), axis=1) > 0.0
        for part in range(2):
            at = slice(part * step, (part + 1) * step)
            query_low, _, _ = normed_rope(q_ref[at], scale_ref[0:1], cosine[at], sine[at])
            scores = jnp.where(live_now, contract_cols(key_low, query_low), masked)
            peak = jnp.max(scores, axis=0, keepdims=True)
            exponent = jnp.exp((scores - peak) * score_scale)
            running = jnp.sum(exponent, axis=0, keepdims=True)
            turned = matmul(value_turned, exponent.astype(bf16)) / running
            out_ref[at] = turned.T.astype(bf16)
            lse_ref[0, :, at] = jnp.broadcast_to(
                peak * score_scale + jnp.log(running), (8, step)
            )

    column = lambda rows: pl.BlockSpec((rows, HEAD), lambda h: (0, h))
    return pl.pallas_call(
        kernel,
        grid=(heads,),
        in_specs=[
            column(queries),
            column(span),
            column(span),
            pl.BlockSpec((2, span, HEAD), lambda h: (0, 0, 0)),
            pl.BlockSpec((8, HEAD), lambda h: (0, 0)),
            pl.BlockSpec((span, HEAD), lambda h: (0, 0)),
        ],
        out_specs=[column(queries), pl.BlockSpec((1, 8, queries), lambda h: (h, 0, 0))],
        out_shape=[
            jax.ShapeDtypeStruct((queries, half), bf16),
            jax.ShapeDtypeStruct((heads, 8, queries), f32),
        ],
        compiler_params=pltpu.CompilerParams(vmem_limit_bytes=VMEM_BYTES),
        name="attention_forward",
    )(query_raw, key_raw, value_low, tables, scales, live)


def attention_backward(query_raw, key_raw, value_low, attended_grad, lse, tables, scales, live):
    queries, half = query_raw.shape
    span = key_raw.shape[0]
    heads = half // HEAD
    step = queries // 2

    def fold(terms):
        return jnp.sum(terms.reshape(-1, 8, HEAD), axis=0)

    def kernel(
        q_ref, k_ref, v_ref, grad_ref, lse_ref, table_ref, scale_ref, live_ref,
        dq_ref, dk_ref, dv_ref, gains_ref,
    ):
        cosine, sine = table_ref[0], table_ref[1]
        key_raw = k_ref[...]
        key_low, key_inverse, _ = normed_rope(key_raw, scale_ref[1:2], cosine, sine)
        key_turned = key_low.astype(f32).T.astype(bf16)
        live_now = jnp.concatenate([live_ref[...]] * (step // HEAD), axis=1) > 0.0
        key_grad = jnp.zeros((span, HEAD), f32)
        value_grad = jnp.zeros((span, HEAD), f32)
        query_gain = jnp.zeros((8, HEAD), f32)
        for part in range(2):
            at = slice(part * step, (part + 1) * step)
            query_raw = q_ref[at]
            query_low, query_inverse, _ = normed_rope(
                query_raw, scale_ref[0:1], cosine[at], sine[at]
            )
            upstream = grad_ref[at]
            scores = jnp.where(
                live_now, contract_cols(key_low, query_low) * score_scale, masked
            )
            probs = jnp.exp(scores - lse_ref[0, 0:1, at])
            probs_grad = contract_cols(v_ref[...], upstream)
            inner = jnp.sum(probs * probs_grad, axis=0, keepdims=True)
            score_grad = (probs * (probs_grad - inner)).astype(bf16)
            value_grad = value_grad + matmul(probs.astype(bf16), upstream)
            key_grad = key_grad + matmul(score_grad, query_low)
            query_grad = matmul(key_turned, score_grad).T * score_scale
            query_grad, terms = rms_back(
                query_raw,
                query_inverse,
                scale_ref[0:1],
                unrope(query_grad, cosine[at], sine[at]),
            )
            dq_ref[at] = query_grad.astype(bf16)
            query_gain = query_gain + fold(terms)
        dv_ref[...] = value_grad.astype(bf16)
        key_grad, terms = rms_back(
            key_raw, key_inverse, scale_ref[1:2], unrope(key_grad * score_scale, cosine, sine)
        )
        dk_ref[...] = key_grad.astype(bf16)
        gains = jnp.stack([query_gain, fold(terms)])

        @pl.when(pl.program_id(0) == 0)
        def _():
            gains_ref[...] = gains

        @pl.when(pl.program_id(0) > 0)
        def _():
            gains_ref[...] = gains_ref[...] + gains

    column = lambda rows: pl.BlockSpec((rows, HEAD), lambda h: (0, h))
    return pl.pallas_call(
        kernel,
        grid=(heads,),
        in_specs=[
            column(queries),
            column(span),
            column(span),
            column(queries),
            pl.BlockSpec((1, 8, queries), lambda h: (h, 0, 0)),
            pl.BlockSpec((2, span, HEAD), lambda h: (0, 0, 0)),
            pl.BlockSpec((8, HEAD), lambda h: (0, 0)),
            pl.BlockSpec((span, HEAD), lambda h: (0, 0)),
        ],
        out_specs=[
            column(queries),
            column(span),
            column(span),
            pl.BlockSpec((2, 8, HEAD), lambda h: (0, 0, 0)),
        ],
        out_shape=[
            jax.ShapeDtypeStruct((queries, half), bf16),
            jax.ShapeDtypeStruct((span, half), bf16),
            jax.ShapeDtypeStruct((span, half), bf16),
            jax.ShapeDtypeStruct((2, 8, HEAD), f32),
        ],
        compiler_params=pltpu.CompilerParams(vmem_limit_bytes=VMEM_BYTES),
        name="attention_backward",
    )(query_raw, key_raw, value_low, attended_grad, lse, tables, scales, live)


def in_order(flag, first, second, axis):
    return jnp.where(
        flag == 0,
        jnp.concatenate([first, second], axis=axis),
        jnp.concatenate([second, first], axis=axis),
    )


def pick(values, start, width, axis=1):
    return lax.dynamic_slice_in_dim(values, start, width, axis=axis)


def split_three(values):
    high = lax.reduce_precision(values, 8, 7)
    rest = values - high
    middle = lax.reduce_precision(rest, 8, 7)
    low = rest - middle
    return (high.astype(bf16), middle.astype(bf16), low.astype(bf16))


def on_device(
    hidden_in,
    prenorm_gain,
    query_weight,
    key_weight,
    value_weight,
    querynorm_gain,
    keynorm_gain,
    output_weight,
    postnorm_gain,
    router_weight,
    expert_inner,
    expert_outer,
    expert_ids,
    pair_order,
    sequence_lengths,
    cotangent,
):
    tokens, width = hidden_in.shape
    owners = lax.axis_size("expert")
    sharers = lax.axis_size("fsdp")
    devices = owners * sharers
    ring = owners // PLANES
    bits = ring.bit_length() - 1
    capacity = tokens * TOPK // owners
    half = width // 2
    owner = lax.axis_index("expert")
    core = lax.axis_index("fsdp")
    parity = owner % 2
    length = lax.dynamic_index_in_dim(sequence_lengths, owner // 2, 0, keepdims=False)

    plane = owner // ring

    def gather_owners(block):
        return lax.all_gather(block, "expert", axis=0, tiled=True)

    def bit_of(b):
        return (owner >> b) & 1

    def gather_planes(block):
        d1, d2, d3 = [swap(block, "expert", d * ring) for d in range(1, PLANES)]
        low, high = plane & 1, plane >> 1
        return in_order(high, in_order(low, block, d1, 0), in_order(low, d2, d3, 0), 0)

    def gather_plane(now, order):
        rows, columns = now.shape[0] // PLANES, now.shape[1]
        now = now.reshape((PLANES,) + (1,) * bits + (rows, columns))
        for b in order:
            now = in_order(bit_of(b), now, swap(now, "expert", 1 << b), bits - b)
        return now.reshape(owners * rows, columns)

    def scatter_steps(left, right, order):
        columns = right.shape[1]
        shape = [PLANES] + [2] * bits + [left.shape[1] // owners]
        axes = list(range(bits))[::-1]

        def halves(values, b, lead):
            at = lead + 1 + axes.index(b)
            return (
                lax.dynamic_index_in_dim(values, bit_of(b), at, keepdims=False),
                lax.dynamic_index_in_dim(values, 1 - bit_of(b), at, keepdims=False),
            )

        stay, go = halves(left.reshape([left.shape[0]] + shape), order[0], 1)
        sent = contract_rows(go.reshape(left.shape[0], -1), right, bf16)
        yield sent
        now = contract_rows(stay.reshape(left.shape[0], -1), right)
        now = now + swap(sent, "expert", 1 << order[0]).astype(f32)
        axes.remove(order[0])
        for b in order[1:]:
            now = now.reshape([PLANES] + [2] * len(axes) + [shape[-1], columns])
            kept, go = halves(now, b, 0)
            axes.remove(b)
            now = kept + swap(go.astype(bf16), "expert", 1 << b).astype(f32)
        now = now.reshape(PLANES, shape[-1], columns)
        total = lax.dynamic_index_in_dim(now, plane, 0, keepdims=False)
        for d in range(1, PLANES):
            sent = lax.dynamic_index_in_dim(now, plane ^ d, 0, keepdims=False)
            total = total + swap(sent.astype(bf16), "expert", d * ring).astype(f32)
        yield total

    descending = list(range(bits))[::-1]
    ascending = list(range(bits))

    def step_up(block, planes):
        return lax.ppermute(
            block, "expert", [(p * ring + i, (p + 1) * ring + i) for p in planes for i in range(ring)]
        )

    def step_down(block, planes):
        return lax.ppermute(
            block, "expert", [(p * ring + i, (p - 1) * ring + i) for p in planes for i in range(ring)]
        )

    rows_dev = width // devices
    small = jnp.concatenate(
        [
            prenorm_gain,
            postnorm_gain,
            querynorm_gain,
            keynorm_gain,
            router_weight.reshape(-1),
        ]
    )
    cut = [0]
    for piece in (prenorm_gain, postnorm_gain, querynorm_gain, keynorm_gain, router_weight):
        cut.append(cut[-1] + piece.size)
    lanes = 128
    small_rows = -(-cut[-1] // (lanes * 16)) * 16
    small = jnp.pad(small, (0, small_rows * lanes - cut[-1])).reshape(small_rows, lanes)
    small_pair = in_order(core, small, swap(small, "fsdp", 1), 0)
    small_all = gather_plane(gather_planes(small_pair), descending)
    small_all = small_all.reshape(devices, small_rows * lanes)
    first_gain = small_all[:, cut[0] : cut[1]].reshape(width).astype(f32)
    second_gain = small_all[:, cut[1] : cut[2]].reshape(width).astype(f32)
    query_scale = small_all[:, cut[2] : cut[3]].reshape(HEAD).astype(f32)
    key_scale = small_all[:, cut[3] : cut[4]].reshape(HEAD).astype(f32)
    router_full = small_all[:, cut[4] : cut[5]].reshape(width, owners)

    other_chip = swap(hidden_in, "expert", 1)
    hidden_own_peer = swap(hidden_in, "fsdp", 1)
    hidden_other_peer = swap(other_chip, "fsdp", 1)
    hidden_seq = jnp.concatenate(
        [hidden_in, hidden_own_peer, other_chip, hidden_other_peer], axis=0
    )

    stacked = jnp.stack([query_weight, key_weight, value_weight, output_weight])
    mine = pick(stacked, core * half, half, axis=2)
    theirs = swap(pick(stacked, (1 - core) * half, half, axis=2), "fsdp", 1)
    shards = in_order(core, mine, theirs, 1)
    query_own = gather_owners(shards[0])
    output_own = gather_owners(shards[3])
    key_first = gather_planes(shards[1])
    value_first = gather_planes(shards[2])

    inner_now = lax.all_gather(expert_inner, "fsdp", axis=1, tiled=True)[0]
    outer_now = lax.all_gather(expert_outer, "fsdp", axis=1, tiled=True)[0]
    extra_width = -(-3 * owners // 128) * 128
    inner_pad = jnp.pad(inner_now, ((0, extra_width), (0, 0)))

    span = 2 * sharers * tokens
    local = jnp.arange(tokens, dtype=jnp.int32)
    positions = jnp.concatenate(
        [
            ((parity ^ a) * sharers + (core ^ c)) * tokens + local
            for a in range(2)
            for c in range(2)
        ]
    )
    token_live = positions[:tokens] < length
    key_live = positions < length
    tables = rotary_tables(positions)
    live_lanes = jnp.broadcast_to(key_live.astype(f32)[:, None], (span, HEAD))
    scales = jnp.pad(jnp.stack([query_scale, key_scale]), ((0, 6), (0, 0)))
    expert_range = jnp.arange(owners, dtype=jnp.int32)
    hot = expert_ids[:, :, None] == expert_range[None, None, :]
    chosen = jnp.any(hot, axis=1)
    far = jnp.int32(1 << 30)
    order_of = jnp.sum(
        jnp.where(hot, pair_order.reshape(tokens, TOPK)[:, :, None], 0), axis=1
    )
    order_of = jnp.where(chosen & token_live[:, None], order_of, far)
    by_expert = order_of.T
    rank_of = jnp.sum(
        (by_expert[:, None, :] < by_expert[:, :, None]).astype(jnp.int32), axis=-1
    ).T
    rank_of = jnp.where(order_of == far, capacity, jnp.minimum(rank_of, capacity))
    kept = (rank_of < capacity).astype(f32)

    def widened(main, extra):
        pad = -extra.shape[1] % 128
        return jnp.concatenate([main, jnp.pad(extra, ((0, 0), (0, pad)))], axis=1)

    upstream_low = jnp.where(token_live[:, None], cotangent, jnp.zeros((), bf16))
    upstream = upstream_low.astype(f32)
    select = (expert_range[:, None] == (owner ^ jnp.arange(ring))[None, :]).astype(bf16)

    last = PLANES - 1

    def by_plane(*choices):
        out = choices[-1]
        for p in reversed(range(len(choices) - 1)):
            out = jnp.where(plane == p, choices[p], out)
        return out

    def planes_of(block):
        up1 = step_up(block, range(last))
        down1 = step_down(block, range(1, PLANES))
        up2 = step_up(up1, range(1, last))
        down2 = step_down(down1, range(1, last))
        up3 = step_up(up2, [2])
        down3 = step_down(down2, [1])
        return [
            block,
            jnp.where(plane == 0, down1, up1),
            by_plane(down2, down1, down1, up2),
            by_plane(down3, down2, up2, up3),
        ]

    def exchange(rows):
        return [rows[:capacity]] + [
            swap(rows[j * capacity : (j + 1) * capacity], "expert", j) for j in range(1, ring)
        ]

    up_wide = widened(upstream_low, rank_of.astype(bf16))
    up_wide, key_first, value_first = lax.optimization_barrier((up_wide, key_first, value_first))
    key_own = gather_plane(key_first, descending)
    value_own = gather_plane(value_first, ascending)
    output_peer = swap(output_own, "fsdp", 1)
    up_planes = planes_of(up_wide)
    up_planes, key_own, value_own = lax.optimization_barrier((up_planes, key_own, value_own))

    def exchange_all(blocks):
        got = [blocks]
        for j in range(1, ring):
            at = slice(j * capacity, (j + 1) * capacity)
            sent = jnp.concatenate([block[at] for block in blocks], axis=0)
            got.append(swap(sent, "expert", j))
        return [
            [blocks[d][:capacity]]
            + [got[j][d * capacity : (d + 1) * capacity] for j in range(1, ring)]
            for d in range(PLANES)
        ]

    pickers, up_picked = [], []
    for d in range(PLANES):
        rank_rel = matmul(up_planes[d][:, width : width + owners], select)
        hits = rank_rel[:, :, None] == jnp.arange(capacity, dtype=f32)[None, None, :]
        picker = hits.astype(bf16).reshape(tokens, ring * capacity)
        pickers.append(picker)
        up_picked.append(contract_rows(picker, up_planes[d][:, :width], bf16))
    up_rows = jnp.concatenate([p for parts in exchange_all(up_picked) for p in parts], axis=0)

    hidden_f = hidden_seq.astype(f32)
    first_normed, first_inverse = rms_scale(hidden_f, first_gain)
    first_low = first_normed.astype(bf16)
    key_raw = matmul(first_low, key_own)
    value_low = matmul(first_low, value_own).astype(bf16)
    query_raw = matmul(first_low[: 2 * tokens], query_own)
    attended, lse = attention_forward(
        query_raw, key_raw, value_low, tables, scales, live_lanes
    )
    attended_cross = swap(attended[tokens:], "fsdp", 1)
    attended_full = in_order(core, attended[:tokens], attended_cross, 1)
    attended_peer = swap(attended_full, "fsdp", 1)
    branch = in_order(
        core, matmul(attended_full, output_own), matmul(attended_full, output_peer), 1
    )
    residual = hidden_in.astype(f32) + branch
    second_normed, second_inverse = rms_scale(residual, second_gain)
    mixed_in = second_normed.astype(bf16)
    logits = matmul(mixed_in, router_full)
    shown = jnp.where(chosen, logits, masked)
    gate_exp = jnp.where(chosen, jnp.exp(shown - jnp.max(shown, axis=-1, keepdims=True)), 0.0)
    gate_soft = gate_exp / jnp.sum(gate_exp, axis=-1, keepdims=True)

    extra = jnp.concatenate(split_three(gate_soft * kept), axis=1)
    in_wide, up_rows = lax.optimization_barrier((widened(mixed_in, extra), up_rows))
    in_planes = planes_of(in_wide)
    column = jnp.arange(extra_width, dtype=jnp.int32)[None, :]
    own_column = (column % owners == owner) & (column < 3 * owners)
    plane_rows = ring * capacity

    hidden_up = contract_cols(up_rows, outer_now)
    row_inputs, hidden_gated, both_grad, rows_back = [], [], [], []
    for d in range(PLANES):
        rows = jnp.concatenate(exchange(contract_rows(pickers[d], in_planes[d], bf16)), axis=0)
        if d:
            rows, rows_back[-1] = lax.optimization_barrier((rows, rows_back[-1]))
        marks = rows[:, width:].astype(f32)
        row_gate = jnp.sum(jnp.where(own_column, marks, 0.0), axis=1, keepdims=True)
        gate_up = matmul(rows, inner_pad)
        up_back = hidden_up[d * plane_rows : (d + 1) * plane_rows]
        gate_part = gate_up[:, :EFF]
        up_part = gate_up[:, EFF:]
        gate_sigmoid = jax.nn.sigmoid(gate_part)
        activated = gate_part * gate_sigmoid
        hidden_rows = activated * up_part
        gated = (hidden_rows * row_gate).astype(bf16)
        row_gate_grad = jnp.sum(hidden_rows * up_back, axis=1, keepdims=True)
        hidden_grad = up_back * row_gate
        grads = jnp.concatenate(
            [
                hidden_grad * up_part * gate_sigmoid * (1.0 + gate_part * (1.0 - gate_sigmoid)),
                hidden_grad * activated,
            ],
            axis=-1,
        ).astype(bf16)
        part_of = jnp.concatenate(
            [jnp.broadcast_to(p, (p.shape[0], owners)) for p in split_three(row_gate_grad)],
            axis=1,
        )
        part_of = jnp.pad(part_of, ((0, 0), (0, extra_width - 3 * owners)))
        part_of = jnp.where(own_column, part_of, jnp.zeros((), bf16))
        rows_back.append(
            contract_cols(grads, inner_pad, bf16) + jnp.pad(part_of, ((0, 0), (width, 0)))
        )
        row_inputs.append(rows[:, :width])
        hidden_gated.append(gated)
        both_grad.append(grads)
    rows_back, row_inputs, hidden_gated, both_grad = lax.optimization_barrier(
        (rows_back, row_inputs, hidden_gated, both_grad)
    )
    rows_out = [matmul(gated, outer_now).astype(bf16) for gated in hidden_gated]
    row_inputs = jnp.concatenate(row_inputs, axis=0)
    hidden_gated = jnp.concatenate(hidden_gated, axis=0)
    both_grad = jnp.concatenate(both_grad, axis=0)

    def bring_back(arrived):
        parts = [None] * PLANES
        for d in reversed(range(PLANES)):
            parts[d] = matmul(pickers[d], jnp.concatenate(arrived[d], axis=0))
        near, middle, far_off = parts[1:]
        end = (plane == 0) | (plane == last)
        send = far_off.astype(bf16)
        up = step_up(send, [0]).astype(f32)
        down = step_down(send, [last]).astype(f32)
        send = jnp.where(end, middle, far_off + up + down).astype(bf16)
        up = step_up(send, [0, 1]).astype(f32)
        down = step_down(send, [2, 3]).astype(f32)
        up = step_up(jnp.where(plane == 0, near, middle + up).astype(bf16), [0, 1, 2])
        down = step_down((near + down).astype(bf16), [1, 2, 3])
        return parts[0] + up.astype(f32) + down.astype(f32)

    eff_half = EFF // 2
    inner_sent = contract_rows(pick(row_inputs, (1 - core) * half, half), both_grad, bf16)
    inner_kept = contract_rows(pick(row_inputs, core * half, half), both_grad)
    outer_sent = contract_rows(
        pick(hidden_gated, (1 - core) * eff_half, eff_half), up_rows, bf16
    )
    outer_kept = contract_rows(pick(hidden_gated, core * eff_half, eff_half), up_rows)
    back = bring_back([exchange(rows) for rows in rows_back])
    back, rows_out, inner_sent, inner_kept, outer_sent, outer_kept = lax.optimization_barrier(
        (back, rows_out, inner_sent, inner_kept, outer_sent, outer_kept)
    )
    inner_grad = inner_kept + swap(inner_sent, "fsdp", 1).astype(f32)
    outer_grad = outer_kept + swap(outer_sent, "fsdp", 1).astype(f32)
    out_arrived = exchange_all(rows_out)
    mixed_grad = back[:, :width]
    gate_grad = (
        back[:, width : width + owners]
        + back[:, width + owners : width + 2 * owners]
        + back[:, width + 2 * owners : width + 3 * owners]
    )

    soft_grad = gate_soft * (gate_grad - jnp.sum(gate_soft * gate_grad, axis=-1, keepdims=True))
    logit_grad = soft_grad.astype(bf16)
    router_local = contract_rows(mixed_in, logit_grad)
    mixed_grad = mixed_grad + contract_cols(logit_grad, router_full)
    residual_part, second_terms = rms_back(residual, second_inverse, second_gain, mixed_grad)
    residual_grad = upstream + residual_part
    branch_low = residual_grad.astype(bf16)
    branch_mine = pick(branch_low, core * half, half)
    branch_theirs = pick(branch_low, (1 - core) * half, half)
    attended_grad = (
        contract_cols(branch_mine, output_own) + contract_cols(branch_theirs, output_peer)
    ).astype(bf16)
    grad_mine = pick(attended_grad, core * half, half)
    grad_cross = swap(pick(attended_grad, (1 - core) * half, half), "fsdp", 1)
    attended_grad = jnp.concatenate([grad_mine, grad_cross], axis=0)

    attended_both = jnp.concatenate([attended_full, attended_peer], axis=0)
    branch_both = jnp.concatenate([branch_mine, swap(branch_theirs, "fsdp", 1)], axis=0)
    output_local = contract_rows(attended_both, branch_both, bf16)

    attended_grad, output_local = lax.optimization_barrier((attended_grad, output_local))
    output_block = lax.psum_scatter(output_local, "expert", scatter_dimension=0, tiled=True)
    output_block = output_block.astype(f32)
    query_low_grad, key_low_grad, value_low_grad, gain_terms = attention_backward(
        query_raw, key_raw, value_low, attended_grad, lse, tables, scales, live_lanes
    )

    out_arrived, query_low_grad, key_low_grad, value_low_grad = lax.optimization_barrier(
        (out_arrived, query_low_grad, key_low_grad, value_low_grad)
    )
    value_steps = scatter_steps(first_low, value_low_grad, descending)
    key_steps = scatter_steps(first_low, key_low_grad, ascending)
    next(value_steps)
    next(key_steps)
    quarter = half // 2
    query_left = first_low[: 2 * tokens]
    query_x = scatter_steps(query_left, query_low_grad[:, :quarter], ascending)
    query_y = scatter_steps(query_left, query_low_grad[:, quarter:], descending)
    next(query_x)
    next(query_y)
    value_block, key_block = next(value_steps), next(key_steps)
    query_block = jnp.concatenate([next(query_x), next(query_y)], axis=1)
    layer_out = (residual + bring_back(out_arrived)).astype(bf16)

    kv_grad = contract_cols(key_low_grad, key_own) + contract_cols(value_low_grad, value_own)
    q_grad = contract_cols(query_low_grad, query_own)
    own_part = kv_grad[:tokens] + q_grad[:tokens]
    peer_part = kv_grad[tokens : 2 * tokens] + q_grad[tokens:]
    far_part = kv_grad[2 * tokens : 3 * tokens]
    far_peer = kv_grad[3 * tokens :]
    crossed = swap(jnp.concatenate([peer_part, far_peer], axis=0).astype(bf16), "fsdp", 1)
    own_part = own_part + crossed[:tokens].astype(f32)
    far_part = (far_part + crossed[tokens:].astype(f32)).astype(bf16)
    far_back = swap(far_part, "expert", 1)
    normed_grad = own_part + far_back.astype(f32)
    hidden_part, first_terms = rms_back(
        hidden_f[:tokens], first_inverse[:tokens], first_gain, normed_grad
    )
    input_grad = residual_grad + hidden_part

    small_grads = jnp.concatenate(
        [
            jnp.sum(first_terms, axis=0).reshape(devices, -1),
            jnp.sum(second_terms, axis=0).reshape(devices, -1),
            jnp.sum(gain_terms[0], axis=0).reshape(devices, -1),
            jnp.sum(gain_terms[1], axis=0).reshape(devices, -1),
            router_local.reshape(devices, -1),
        ],
        axis=1,
    )
    small_grads = jnp.pad(small_grads, ((0, 0), (0, small_rows * lanes - cut[-1])))
    now = small_grads.reshape([PLANES] + [2] * bits + [2, small_rows, lanes])
    at = bits + 1
    sent = lax.dynamic_index_in_dim(now, 1 - core, at, keepdims=False)
    now = lax.dynamic_index_in_dim(now, core, at, keepdims=False) + swap(sent, "fsdp", 1)
    for b in range(bits):
        at = bits - b
        sent = lax.dynamic_index_in_dim(now, 1 - bit_of(b), at, keepdims=False)
        now = lax.dynamic_index_in_dim(now, bit_of(b), at, keepdims=False) + swap(
            sent, "expert", 1 << b
        )
    small_sum = lax.dynamic_index_in_dim(now, plane, 0, keepdims=False)
    for d in range(1, PLANES):
        sent = lax.dynamic_index_in_dim(now, plane ^ d, 0, keepdims=False)
        small_sum = small_sum + swap(sent, "expert", d * ring)
    small_sum = small_sum.reshape(-1)

    def whole_rows(block):
        keep = pick(block, core * rows_dev, rows_dev, 0)
        cross = swap(pick(block, (1 - core) * rows_dev, rows_dev, 0), "fsdp", 1)
        return in_order(core, keep, cross, 1)

    weight_grads = [whole_rows(b) for b in (query_block, key_block, value_block, output_block)]
    return (
        layer_out,
        input_grad,
        small_sum[cut[0] : cut[1]],
        weight_grads[0],
        weight_grads[1],
        weight_grads[2],
        small_sum[cut[2] : cut[3]],
        small_sum[cut[3] : cut[4]],
        weight_grads[3],
        small_sum[cut[1] : cut[2]],
        small_sum[cut[4] : cut[5]].reshape(rows_dev, owners),
        inner_grad[None],
        outer_grad[None],
    )


def solution(mesh):
    both = ("expert", "fsdp")
    placed = (
        P(both, None),
        P(both),
        P(both, None),
        P(both, None),
        P(both, None),
        P(both),
        P(both),
        P(both, None),
        P(both),
        P(both, None),
        P("expert", "fsdp", None),
        P("expert", "fsdp", None),
        P(both, None),
        P(both, None),
        P(),
        P(both, None),
    )
    return jax.shard_map(
        on_device,
        mesh=mesh,
        in_specs=placed,
        out_specs=(
            P(both, None),
            P(both, None),
            P(both),
            P(both, None),
            P(both, None),
            P(both, None),
            P(both),
            P(both),
            P(both, None),
            P(both),
            P(both, None),
            P("expert", "fsdp", None),
            P("expert", "fsdp", None),
        ),
        check_vma=False,
    )
```

```python
import math

import jax
import jax.numpy as jnp
from jax import lax
from jax.experimental import pallas as pl
from jax.experimental.pallas import tpu as pltpu
from jax.sharding import PartitionSpec as P

HEAD = 128
EFF = 1024
TOPK = 8
PLANES = 4

epsilon = 1e-06
rope_base = 10000.0
masked = -1e30
bf16 = jnp.bfloat16
f32 = jnp.float32
score_scale = 1.0 / math.sqrt(HEAD)
VMEM_BYTES = 40 * 1024 * 1024


def swap(block, axis, mask):
    count = lax.axis_size(axis)
    return lax.ppermute(block, axis, [(i, i ^ mask) for i in range(count)])


def contract_rows(left, right, out=f32):
    return lax.dot_general(
        left, right, (((0,), (0,)), ((), ())), preferred_element_type=f32
    ).astype(out)


def contract_cols(left, right, out=f32):
    return lax.dot_general(
        left, right, (((1,), (1,)), ((), ())), preferred_element_type=f32
    ).astype(out)


def matmul(left, right):
    return jnp.dot(left, right, preferred_element_type=f32)


def rms_scale(values, gain):
    inverse = lax.rsqrt(jnp.mean(values * values, axis=-1, keepdims=True) + epsilon)
    return (values * inverse * gain, inverse)


def rms_back(values, inverse, gain, upstream):
    scaled = upstream * gain
    inner_sum = jnp.sum(scaled * values, axis=-1, keepdims=True)
    length_now = values.shape[-1]
    grad_values = inverse * scaled - values * (inverse * inverse * inverse) * (
        inner_sum / length_now
    )
    return (grad_values, upstream * values * inverse)


def rotary_tables(positions):
    half_width = HEAD // 2
    freq_steps = jnp.arange(half_width, dtype=f32)
    frequency = jnp.exp(freq_steps * (-2.0 * math.log(rope_base) / HEAD))
    angles = positions.astype(f32)[:, None] * frequency[None, :]
    cosine, sine = jnp.cos(angles), jnp.sin(angles)
    return jnp.stack(
        [
            jnp.concatenate([cosine, cosine], axis=-1),
            jnp.concatenate([-sine, sine], axis=-1),
        ]
    )


def unrope(upstream, cosine, sine):
    return upstream * cosine - pltpu.roll(upstream, HEAD // 2, 1) * sine


def normed_rope(values, gain, cosine, sine):
    normed, inverse = rms_scale(values, gain)
    turned = normed * cosine + pltpu.roll(normed, HEAD // 2, 1) * sine
    return turned.astype(bf16), inverse, normed


def attention_forward(query_raw, key_raw, value_low, tables, scales, live):
    queries, half = query_raw.shape
    span = key_raw.shape[0]
    heads = half // HEAD
    step = queries // 2

    def kernel(q_ref, k_ref, v_ref, table_ref, scale_ref, live_ref, out_ref, lse_ref):
        cosine, sine = table_ref[0], table_ref[1]
        key_low, _, _ = normed_rope(k_ref[...], scale_ref[1:2], cosine, sine)
        value_turned = v_ref[...].astype(f32).T.astype(bf16)
        live_now = jnp.concatenate([live_ref[...]] * (step // HEAD), axis=1) > 0.0
        for part in range(2):
            at = slice(part * step, (part + 1) * step)
            query_low, _, _ = normed_rope(q_ref[at], scale_ref[0:1], cosine[at], sine[at])
            scores = jnp.where(live_now, contract_cols(key_low, query_low), masked)
            peak = jnp.max(scores, axis=0, keepdims=True)
            exponent = jnp.exp((scores - peak) * score_scale)
            running = jnp.sum(exponent, axis=0, keepdims=True)
            turned = matmul(value_turned, exponent.astype(bf16)) / running
            out_ref[at] = turned.T.astype(bf16)
            lse_ref[0, :, at] = jnp.broadcast_to(
                peak * score_scale + jnp.log(running), (8, step)
            )

    column = lambda rows: pl.BlockSpec((rows, HEAD), lambda h: (0, h))
    return pl.pallas_call(
        kernel,
        grid=(heads,),
        in_specs=[
            column(queries),
            column(span),
            column(span),
            pl.BlockSpec((2, span, HEAD), lambda h: (0, 0, 0)),
            pl.BlockSpec((8, HEAD), lambda h: (0, 0)),
            pl.BlockSpec((span, HEAD), lambda h: (0, 0)),
        ],
        out_specs=[column(queries), pl.BlockSpec((1, 8, queries), lambda h: (h, 0, 0))],
        out_shape=[
            jax.ShapeDtypeStruct((queries, half), bf16),
            jax.ShapeDtypeStruct((heads, 8, queries), f32),
        ],
        compiler_params=pltpu.CompilerParams(vmem_limit_bytes=VMEM_BYTES),
        name="attention_forward",
    )(query_raw, key_raw, value_low, tables, scales, live)


def attention_backward(query_raw, key_raw, value_low, attended_grad, lse, tables, scales, live):
    queries, half = query_raw.shape
    span = key_raw.shape[0]
    heads = half // HEAD
    step = queries // 2

    def fold(terms):
        return jnp.sum(terms.reshape(-1, 8, HEAD), axis=0)

    def kernel(
        q_ref, k_ref, v_ref, grad_ref, lse_ref, table_ref, scale_ref, live_ref,
        dq_ref, dk_ref, dv_ref, gains_ref,
    ):
        cosine, sine = table_ref[0], table_ref[1]
        key_raw = k_ref[...]
        key_low, key_inverse, _ = normed_rope(key_raw, scale_ref[1:2], cosine, sine)
        key_turned = key_low.astype(f32).T.astype(bf16)
        live_now = jnp.concatenate([live_ref[...]] * (step // HEAD), axis=1) > 0.0
        key_grad = jnp.zeros((span, HEAD), f32)
        value_grad = jnp.zeros((span, HEAD), f32)
        query_gain = jnp.zeros((8, HEAD), f32)
        for part in range(2):
            at = slice(part * step, (part + 1) * step)
            query_raw = q_ref[at]
            query_low, query_inverse, _ = normed_rope(
                query_raw, scale_ref[0:1], cosine[at], sine[at]
            )
            upstream = grad_ref[at]
            scores = jnp.where(
                live_now, contract_cols(key_low, query_low) * score_scale, masked
            )
            probs = jnp.exp(scores - lse_ref[0, 0:1, at])
            probs_grad = contract_cols(v_ref[...], upstream)
            inner = jnp.sum(probs * probs_grad, axis=0, keepdims=True)
            score_grad = (probs * (probs_grad - inner)).astype(bf16)
            value_grad = value_grad + matmul(probs.astype(bf16), upstream)
            key_grad = key_grad + matmul(score_grad, query_low)
            query_grad = matmul(key_turned, score_grad).T * score_scale
            query_grad, terms = rms_back(
                query_raw,
                query_inverse,
                scale_ref[0:1],
                unrope(query_grad, cosine[at], sine[at]),
            )
            dq_ref[at] = query_grad.astype(bf16)
            query_gain = query_gain + fold(terms)
        dv_ref[...] = value_grad.astype(bf16)
        key_grad, terms = rms_back(
            key_raw, key_inverse, scale_ref[1:2], unrope(key_grad * score_scale, cosine, sine)
        )
        dk_ref[...] = key_grad.astype(bf16)
        gains = jnp.stack([query_gain, fold(terms)])

        @pl.when(pl.program_id(0) == 0)
        def _():
            gains_ref[...] = gains

        @pl.when(pl.program_id(0) > 0)
        def _():
            gains_ref[...] = gains_ref[...] + gains

    column = lambda rows: pl.BlockSpec((rows, HEAD), lambda h: (0, h))
    return pl.pallas_call(
        kernel,
        grid=(heads,),
        in_specs=[
            column(queries),
            column(span),
            column(span),
            column(queries),
            pl.BlockSpec((1, 8, queries), lambda h: (h, 0, 0)),
            pl.BlockSpec((2, span, HEAD), lambda h: (0, 0, 0)),
            pl.BlockSpec((8, HEAD), lambda h: (0, 0)),
            pl.BlockSpec((span, HEAD), lambda h: (0, 0)),
        ],
        out_specs=[
            column(queries),
            column(span),
            column(span),
            pl.BlockSpec((2, 8, HEAD), lambda h: (0, 0, 0)),
        ],
        out_shape=[
            jax.ShapeDtypeStruct((queries, half), bf16),
            jax.ShapeDtypeStruct((span, half), bf16),
            jax.ShapeDtypeStruct((span, half), bf16),
            jax.ShapeDtypeStruct((2, 8, HEAD), f32),
        ],
        compiler_params=pltpu.CompilerParams(vmem_limit_bytes=VMEM_BYTES),
        name="attention_backward",
    )(query_raw, key_raw, value_low, attended_grad, lse, tables, scales, live)


def in_order(flag, first, second, axis):
    return jnp.where(
        flag == 0,
        jnp.concatenate([first, second], axis=axis),
        jnp.concatenate([second, first], axis=axis),
    )


def pick(values, start, width, axis=1):
    return lax.dynamic_slice_in_dim(values, start, width, axis=axis)


def split_three(values):
    high = lax.reduce_precision(values, 8, 7)
    rest = values - high
    middle = lax.reduce_precision(rest, 8, 7)
    low = rest - middle
    return (high.astype(bf16), middle.astype(bf16), low.astype(bf16))


def on_device(
    hidden_in,
    prenorm_gain,
    query_weight,
    key_weight,
    value_weight,
    querynorm_gain,
    keynorm_gain,
    output_weight,
    postnorm_gain,
    router_weight,
    expert_inner,
    expert_outer,
    expert_ids,
    pair_order,
    sequence_lengths,
    cotangent,
):
    tokens, width = hidden_in.shape
    owners = lax.axis_size("expert")
    sharers = lax.axis_size("fsdp")
    devices = owners * sharers
    ring = owners // PLANES
    bits = ring.bit_length() - 1
    capacity = tokens * TOPK // owners
    half = width // 2
    owner = lax.axis_index("expert")
    core = lax.axis_index("fsdp")
    parity = owner % 2
    length = lax.dynamic_index_in_dim(sequence_lengths, owner // 2, 0, keepdims=False)

    plane = owner // ring

    def gather_owners(block):
        return lax.all_gather(block, "expert", axis=0, tiled=True)

    def bit_of(b):
        return (owner >> b) & 1

    def gather_planes(block):
        d1, d2, d3 = [swap(block, "expert", d * ring) for d in range(1, PLANES)]
        low, high = plane & 1, plane >> 1
        return in_order(high, in_order(low, block, d1, 0), in_order(low, d2, d3, 0), 0)

    def gather_plane(now, order):
        rows, columns = now.shape[0] // PLANES, now.shape[1]
        now = now.reshape((PLANES,) + (1,) * bits + (rows, columns))
        for b in order:
            now = in_order(bit_of(b), now, swap(now, "expert", 1 << b), bits - b)
        return now.reshape(owners * rows, columns)

    def split_columns(values, b):
        each = values.shape[1] // owners

        def side(bit):
            return jnp.concatenate(
                [
                    pick(values, ((k << (b + 1)) + (bit << b)) * each, each << b)
                    for k in range(owners >> (b + 1))
                ],
                axis=1,
            )

        return side(bit_of(b)), side(1 - bit_of(b))

    def scatter_rest(stay, right, arrived, order):
        columns = right.shape[1]
        now = contract_rows(stay, right) + arrived.astype(f32)
        axes = [b for b in reversed(range(bits)) if b != order[0]]
        rows = width // owners
        for b in order[1:]:
            now = now.reshape([PLANES] + [2] * len(axes) + [rows, columns])
            at = 1 + axes.index(b)
            kept = lax.dynamic_index_in_dim(now, bit_of(b), at, keepdims=False)
            sent = lax.dynamic_index_in_dim(now, 1 - bit_of(b), at, keepdims=False)
            axes.remove(b)
            now = kept + swap(sent.astype(bf16), "expert", 1 << b).astype(f32)
        return now.reshape(PLANES, rows, columns)

    def scatter_planes(now):
        total = lax.dynamic_index_in_dim(now, plane, 0, keepdims=False)
        for d in range(1, PLANES):
            sent = lax.dynamic_index_in_dim(now, plane ^ d, 0, keepdims=False)
            total = total + swap(sent.astype(bf16), "expert", d * ring).astype(f32)
        return total

    descending = list(range(bits))[::-1]
    ascending = list(range(bits))

    def step_up(block, planes):
        return lax.ppermute(
            block, "expert", [(p * ring + i, (p + 1) * ring + i) for p in planes for i in range(ring)]
        )

    def step_down(block, planes):
        return lax.ppermute(
            block, "expert", [(p * ring + i, (p - 1) * ring + i) for p in planes for i in range(ring)]
        )

    rows_dev = width // devices
    small = jnp.concatenate(
        [
            prenorm_gain,
            postnorm_gain,
            querynorm_gain,
            keynorm_gain,
            router_weight.reshape(-1),
        ]
    )
    cut = [0]
    for piece in (prenorm_gain, postnorm_gain, querynorm_gain, keynorm_gain, router_weight):
        cut.append(cut[-1] + piece.size)
    lanes = 128
    small_rows = -(-cut[-1] // (lanes * 16)) * 16
    small = jnp.pad(small, (0, small_rows * lanes - cut[-1])).reshape(small_rows, lanes)
    small_pair = in_order(core, small, swap(small, "fsdp", 1), 0)
    small_all = gather_plane(gather_planes(small_pair), descending)
    small_all = small_all.reshape(devices, small_rows * lanes)
    first_gain = small_all[:, cut[0] : cut[1]].reshape(width).astype(f32)
    second_gain = small_all[:, cut[1] : cut[2]].reshape(width).astype(f32)
    query_scale = small_all[:, cut[2] : cut[3]].reshape(HEAD).astype(f32)
    key_scale = small_all[:, cut[3] : cut[4]].reshape(HEAD).astype(f32)
    router_full = small_all[:, cut[4] : cut[5]].reshape(width, owners)

    other_chip = swap(hidden_in, "expert", 1)
    hidden_own_peer = swap(hidden_in, "fsdp", 1)
    hidden_other_peer = swap(other_chip, "fsdp", 1)
    hidden_seq = jnp.concatenate(
        [hidden_in, hidden_own_peer, other_chip, hidden_other_peer], axis=0
    )

    stacked = jnp.stack([query_weight, key_weight, value_weight, output_weight])
    mine = pick(stacked, core * half, half, axis=2)
    theirs = swap(pick(stacked, (1 - core) * half, half, axis=2), "fsdp", 1)
    shards = in_order(core, mine, theirs, 1)
    query_own = gather_owners(shards[0])
    output_own = gather_owners(shards[3])
    key_first = gather_planes(shards[1])
    value_first = gather_planes(shards[2])

    inner_now = lax.all_gather(expert_inner, "fsdp", axis=1, tiled=True)[0]
    outer_now = lax.all_gather(expert_outer, "fsdp", axis=1, tiled=True)[0]
    extra_width = -(-3 * owners // 128) * 128
    inner_pad = jnp.pad(inner_now, ((0, extra_width), (0, 0)))

    span = 2 * sharers * tokens
    local = jnp.arange(tokens, dtype=jnp.int32)
    positions = jnp.concatenate(
        [
            ((parity ^ a) * sharers + (core ^ c)) * tokens + local
            for a in range(2)
            for c in range(2)
        ]
    )
    token_live = positions[:tokens] < length
    key_live = positions < length
    tables = rotary_tables(positions)
    live_lanes = jnp.broadcast_to(key_live.astype(f32)[:, None], (span, HEAD))
    scales = jnp.pad(jnp.stack([query_scale, key_scale]), ((0, 6), (0, 0)))
    expert_range = jnp.arange(owners, dtype=jnp.int32)
    hot = expert_ids[:, :, None] == expert_range[None, None, :]
    chosen = jnp.any(hot, axis=1)
    far = jnp.int32(1 << 30)
    order_of = jnp.sum(
        jnp.where(hot, pair_order.reshape(tokens, TOPK)[:, :, None], 0), axis=1
    )
    order_of = jnp.where(chosen & token_live[:, None], order_of, far)
    by_expert = order_of.T
    rank_of = jnp.sum(
        (by_expert[:, None, :] < by_expert[:, :, None]).astype(jnp.int32), axis=-1
    ).T
    rank_of = jnp.where(order_of == far, capacity, jnp.minimum(rank_of, capacity))
    kept = (rank_of < capacity).astype(f32)

    def widened(main, extra):
        pad = -extra.shape[1] % 128
        return jnp.concatenate([main, jnp.pad(extra, ((0, 0), (0, pad)))], axis=1)

    upstream_low = jnp.where(token_live[:, None], cotangent, jnp.zeros((), bf16))
    upstream = upstream_low.astype(f32)
    select = (expert_range[:, None] == (owner ^ jnp.arange(ring))[None, :]).astype(bf16)

    last = PLANES - 1

    def by_plane(*choices):
        out = choices[-1]
        for p in reversed(range(len(choices) - 1)):
            out = jnp.where(plane == p, choices[p], out)
        return out

    def planes_of(block):
        up1 = step_up(block, range(last))
        down1 = step_down(block, range(1, PLANES))
        up2 = step_up(up1, range(1, last))
        down2 = step_down(down1, range(1, last))
        up3 = step_up(up2, [2])
        down3 = step_down(down2, [1])
        return [
            block,
            jnp.where(plane == 0, down1, up1),
            by_plane(down2, down1, down1, up2),
            by_plane(down3, down2, up2, up3),
        ]

    def exchange(rows):
        return [rows[:capacity]] + [
            swap(rows[j * capacity : (j + 1) * capacity], "expert", j) for j in range(1, ring)
        ]

    up_wide = widened(upstream_low, rank_of.astype(bf16))
    up_wide, key_first, value_first = lax.optimization_barrier((up_wide, key_first, value_first))
    key_own = gather_plane(key_first, descending)
    value_own = gather_plane(value_first, ascending)
    output_peer = swap(output_own, "fsdp", 1)
    up_planes = planes_of(up_wide)
    up_planes, key_late, value_late = lax.optimization_barrier((up_planes, key_own, value_own))

    def exchange_all(blocks):
        got = [blocks]
        for j in range(1, ring):
            at = slice(j * capacity, (j + 1) * capacity)
            sent = jnp.concatenate([block[at] for block in blocks], axis=0)
            got.append(swap(sent, "expert", j))
        return [
            [blocks[d][:capacity]]
            + [got[j][d * capacity : (d + 1) * capacity] for j in range(1, ring)]
            for d in range(PLANES)
        ]

    pickers, up_picked = [], []
    for d in range(PLANES):
        rank_rel = matmul(up_planes[d][:, width : width + owners], select)
        hits = rank_rel[:, :, None] == jnp.arange(capacity, dtype=f32)[None, None, :]
        picker = hits.astype(bf16).reshape(tokens, ring * capacity)
        pickers.append(picker)
        up_picked.append(contract_rows(picker, up_planes[d][:, :width], bf16))
    up_arrived = exchange_all(up_picked)

    hidden_f = hidden_seq.astype(f32)
    first_normed, first_inverse = rms_scale(hidden_f, first_gain)
    first_low = first_normed.astype(bf16)
    key_raw = matmul(first_low, key_own)
    value_low = matmul(first_low, value_own).astype(bf16)
    query_raw = matmul(first_low[: 2 * tokens], query_own)
    attended, lse = attention_forward(
        query_raw, key_raw, value_low, tables, scales, live_lanes
    )
    left_x = split_columns(first_low, 0)
    left_y = split_columns(first_low, bits - 1)
    attended_cross = swap(attended[tokens:], "fsdp", 1)
    attended_full = in_order(core, attended[:tokens], attended_cross, 1)
    attended_peer = swap(attended_full, "fsdp", 1)
    branch = in_order(
        core, matmul(attended_full, output_own), matmul(attended_full, output_peer), 1
    )
    residual = hidden_in.astype(f32) + branch
    second_normed, second_inverse = rms_scale(residual, second_gain)
    mixed_in = second_normed.astype(bf16)
    logits = matmul(mixed_in, router_full)
    shown = jnp.where(chosen, logits, masked)
    gate_exp = jnp.where(chosen, jnp.exp(shown - jnp.max(shown, axis=-1, keepdims=True)), 0.0)
    gate_soft = gate_exp / jnp.sum(gate_exp, axis=-1, keepdims=True)

    extra = jnp.concatenate(split_three(gate_soft * kept), axis=1)
    in_planes = planes_of(widened(mixed_in, extra))
    up_arrived, mixed_late = lax.optimization_barrier((up_arrived, mixed_in))
    up_rows = jnp.concatenate([p for parts in up_arrived for p in parts], axis=0)
    picked = [contract_rows(pickers[d], in_planes[d], bf16) for d in range(PLANES)]
    picked[0], up_rows = lax.optimization_barrier((picked[0], up_rows))
    column = jnp.arange(extra_width, dtype=jnp.int32)[None, :]
    own_column = (column % owners == owner) & (column < 3 * owners)
    plane_rows = ring * capacity

    hidden_up = contract_cols(up_rows, outer_now)
    row_inputs, hidden_gated, both_grad, rows_back = [], [], [], []
    for d in range(PLANES):
        rows = exchange(picked[d])
        if d < last:
            rows, picked[d + 1] = lax.optimization_barrier((rows, picked[d + 1]))
        if d == 0:
            rows, left_x, left_y = lax.optimization_barrier((rows, left_x, left_y))
        rows = jnp.concatenate(rows, axis=0)
        if d:
            rows, rows_back[-1] = lax.optimization_barrier((rows, rows_back[-1]))
        marks = rows[:, width:].astype(f32)
        row_gate = jnp.sum(jnp.where(own_column, marks, 0.0), axis=1, keepdims=True)
        gate_up = matmul(rows, inner_pad)
        up_back = hidden_up[d * plane_rows : (d + 1) * plane_rows]
        gate_part = gate_up[:, :EFF]
        up_part = gate_up[:, EFF:]
        gate_sigmoid = jax.nn.sigmoid(gate_part)
        activated = gate_part * gate_sigmoid
        hidden_rows = activated * up_part
        gated = (hidden_rows * row_gate).astype(bf16)
        row_gate_grad = jnp.sum(hidden_rows * up_back, axis=1, keepdims=True)
        hidden_grad = up_back * row_gate
        grads = jnp.concatenate(
            [
                hidden_grad * up_part * gate_sigmoid * (1.0 + gate_part * (1.0 - gate_sigmoid)),
                hidden_grad * activated,
            ],
            axis=-1,
        ).astype(bf16)
        part_of = jnp.concatenate(
            [jnp.broadcast_to(p, (p.shape[0], owners)) for p in split_three(row_gate_grad)],
            axis=1,
        )
        part_of = jnp.pad(part_of, ((0, 0), (0, extra_width - 3 * owners)))
        part_of = jnp.where(own_column, part_of, jnp.zeros((), bf16))
        rows_back.append(
            contract_cols(grads, inner_pad, bf16) + jnp.pad(part_of, ((0, 0), (width, 0)))
        )
        row_inputs.append(rows[:, :width])
        hidden_gated.append(gated)
        both_grad.append(grads)
    arrived = [None] * PLANES
    for d in reversed(range(PLANES)):
        block = rows_back[d]
        if d < last:
            block, arrived[d + 1] = lax.optimization_barrier((block, arrived[d + 1]))
        arrived[d] = exchange(block)
    arrived[last], row_inputs, hidden_gated, both_grad = lax.optimization_barrier(
        (arrived[last], row_inputs, hidden_gated, both_grad)
    )
    rows_out = [matmul(gated, outer_now).astype(bf16) for gated in hidden_gated]
    row_inputs = jnp.concatenate(row_inputs, axis=0)
    hidden_gated = jnp.concatenate(hidden_gated, axis=0)
    both_grad = jnp.concatenate(both_grad, axis=0)

    def bring_back(arrived):
        parts = [None] * PLANES
        for d in reversed(range(PLANES)):
            parts[d] = matmul(pickers[d], jnp.concatenate(arrived[d], axis=0))
        near, middle, far_off = parts[1:]
        end = (plane == 0) | (plane == last)
        send = far_off.astype(bf16)
        up = step_up(send, [0]).astype(f32)
        down = step_down(send, [last]).astype(f32)
        send = jnp.where(end, middle, far_off + up + down).astype(bf16)
        up = step_up(send, [0, 1]).astype(f32)
        down = step_down(send, [2, 3]).astype(f32)
        up = step_up(jnp.where(plane == 0, near, middle + up).astype(bf16), [0, 1, 2])
        down = step_down((near + down).astype(bf16), [1, 2, 3])
        return parts[0] + up.astype(f32) + down.astype(f32)

    eff_half = EFF // 2
    inner_sent = contract_rows(pick(row_inputs, (1 - core) * half, half), both_grad, bf16)
    inner_kept = contract_rows(pick(row_inputs, core * half, half), both_grad)
    outer_sent = contract_rows(
        pick(hidden_gated, (1 - core) * eff_half, eff_half), up_rows, bf16
    )
    outer_kept = contract_rows(pick(hidden_gated, core * eff_half, eff_half), up_rows)
    back = bring_back(arrived)
    back, rows_out, inner_sent, inner_kept, outer_sent, outer_kept = lax.optimization_barrier(
        (back, rows_out, inner_sent, inner_kept, outer_sent, outer_kept)
    )
    inner_grad = inner_kept + swap(inner_sent, "fsdp", 1).astype(f32)
    outer_grad = outer_kept + swap(outer_sent, "fsdp", 1).astype(f32)
    out_arrived = exchange_all(rows_out)
    mixed_grad = back[:, :width]
    gate_grad = (
        back[:, width : width + owners]
        + back[:, width + owners : width + 2 * owners]
        + back[:, width + 2 * owners : width + 3 * owners]
    )

    soft_grad = gate_soft * (gate_grad - jnp.sum(gate_soft * gate_grad, axis=-1, keepdims=True))
    logit_grad = soft_grad.astype(bf16)
    router_local = contract_rows(mixed_late, logit_grad)
    mixed_grad = mixed_grad + contract_cols(logit_grad, router_full)
    residual_part, second_terms = rms_back(residual, second_inverse, second_gain, mixed_grad)
    residual_grad = upstream + residual_part
    branch_low = residual_grad.astype(bf16)
    branch_mine = pick(branch_low, core * half, half)
    branch_theirs = pick(branch_low, (1 - core) * half, half)
    attended_grad = (
        contract_cols(branch_mine, output_own) + contract_cols(branch_theirs, output_peer)
    ).astype(bf16)
    grad_mine = pick(attended_grad, core * half, half)
    grad_cross = swap(pick(attended_grad, (1 - core) * half, half), "fsdp", 1)
    attended_grad = jnp.concatenate([grad_mine, grad_cross], axis=0)

    attended_both = jnp.concatenate([attended_full, attended_peer], axis=0)
    branch_both = jnp.concatenate([branch_mine, swap(branch_theirs, "fsdp", 1)], axis=0)
    output_local = contract_rows(attended_both, branch_both, bf16)

    attended_grad, output_local = lax.optimization_barrier((attended_grad, output_local))
    output_block = lax.psum_scatter(output_local, "expert", scatter_dimension=0, tiled=True)
    output_block = output_block.astype(f32)
    query_low_grad, key_low_grad, value_low_grad, gain_terms = attention_backward(
        query_raw, key_raw, value_low, attended_grad, lse, tables, scales, live_lanes
    )

    out_arrived, query_low_grad, key_low_grad, value_low_grad = lax.optimization_barrier(
        (out_arrived, query_low_grad, key_low_grad, value_low_grad)
    )
    quarter = half // 2
    chip = 2 * tokens
    sent = [
        contract_rows(left_y[1], value_low_grad, bf16),
        contract_rows(left_x[1], key_low_grad, bf16),
    ]
    sent, query_low_grad = lax.optimization_barrier((sent, query_low_grad))
    sent += [
        contract_rows(left_x[1][:chip], query_low_grad[:, :quarter], bf16),
        contract_rows(left_y[1][:chip], query_low_grad[:, quarter:], bf16),
    ]
    sent, query_late, key_grad_late, value_grad_late = lax.optimization_barrier(
        (sent, query_low_grad, key_low_grad, value_low_grad)
    )
    value_came = swap(sent[0], "expert", 1 << (bits - 1))
    key_came = swap(sent[1], "expert", 1)
    out_arrived, value_came, key_came = lax.optimization_barrier(
        (out_arrived, value_came, key_came)
    )
    sent, value_came, key_came = lax.optimization_barrier((sent, value_came, key_came))
    query_x_came = swap(sent[2], "expert", 1)
    query_y_came = swap(sent[3], "expert", 1 << (bits - 1))
    value_block = scatter_planes(scatter_rest(left_y[0], value_low_grad, value_came, descending))
    key_block = scatter_planes(scatter_rest(left_x[0], key_low_grad, key_came, ascending))
    query_block = scatter_planes(
        jnp.concatenate(
            [
                scatter_rest(
                    left_x[0][:chip], query_low_grad[:, :quarter], query_x_came, ascending
                ),
                scatter_rest(
                    left_y[0][:chip], query_low_grad[:, quarter:], query_y_came, descending
                ),
            ],
            axis=2,
        )
    )
    layer_out = (residual + bring_back(out_arrived)).astype(bf16)

    kv_grad = contract_cols(key_grad_late, key_late) + contract_cols(value_grad_late, value_late)
    q_grad = contract_cols(query_late, query_own)
    own_part = kv_grad[:tokens] + q_grad[:tokens]
    peer_part = kv_grad[tokens : 2 * tokens] + q_grad[tokens:]
    far_part = kv_grad[2 * tokens : 3 * tokens]
    far_peer = kv_grad[3 * tokens :]
    crossed = swap(jnp.concatenate([peer_part, far_peer], axis=0).astype(bf16), "fsdp", 1)
    own_part = own_part + crossed[:tokens].astype(f32)
    far_part = (far_part + crossed[tokens:].astype(f32)).astype(bf16)
    far_back = swap(far_part, "expert", 1)
    normed_grad = own_part + far_back.astype(f32)
    hidden_part, first_terms = rms_back(
        hidden_f[:tokens], first_inverse[:tokens], first_gain, normed_grad
    )
    input_grad = residual_grad + hidden_part

    small_grads = jnp.concatenate(
        [
            jnp.sum(first_terms, axis=0).reshape(devices, -1),
            jnp.sum(second_terms, axis=0).reshape(devices, -1),
            jnp.sum(gain_terms[0], axis=0).reshape(devices, -1),
            jnp.sum(gain_terms[1], axis=0).reshape(devices, -1),
            router_local.reshape(devices, -1),
        ],
        axis=1,
    )
    small_grads = jnp.pad(small_grads, ((0, 0), (0, small_rows * lanes - cut[-1])))
    now = small_grads.reshape([PLANES] + [2] * bits + [2, small_rows, lanes])
    at = bits + 1
    sent = lax.dynamic_index_in_dim(now, 1 - core, at, keepdims=False)
    now = lax.dynamic_index_in_dim(now, core, at, keepdims=False) + swap(sent, "fsdp", 1)
    for b in range(bits):
        at = bits - b
        sent = lax.dynamic_index_in_dim(now, 1 - bit_of(b), at, keepdims=False)
        now = lax.dynamic_index_in_dim(now, bit_of(b), at, keepdims=False) + swap(
            sent, "expert", 1 << b
        )
    small_sum = lax.dynamic_index_in_dim(now, plane, 0, keepdims=False)
    for d in range(1, PLANES):
        sent = lax.dynamic_index_in_dim(now, plane ^ d, 0, keepdims=False)
        small_sum = small_sum + swap(sent, "expert", d * ring)
    small_sum = small_sum.reshape(-1)

    def whole_rows(block):
        keep = pick(block, core * rows_dev, rows_dev, 0)
        cross = swap(pick(block, (1 - core) * rows_dev, rows_dev, 0), "fsdp", 1)
        return in_order(core, keep, cross, 1)

    weight_grads = [whole_rows(b) for b in (query_block, key_block, value_block, output_block)]
    return (
        layer_out,
        input_grad,
        small_sum[cut[0] : cut[1]],
        weight_grads[0],
        weight_grads[1],
        weight_grads[2],
        small_sum[cut[2] : cut[3]],
        small_sum[cut[3] : cut[4]],
        weight_grads[3],
        small_sum[cut[1] : cut[2]],
        small_sum[cut[4] : cut[5]].reshape(rows_dev, owners),
        inner_grad[None],
        outer_grad[None],
    )


def solution(mesh):
    both = ("expert", "fsdp")
    placed = (
        P(both, None),
        P(both),
        P(both, None),
        P(both, None),
        P(both, None),
        P(both),
        P(both),
        P(both, None),
        P(both),
        P(both, None),
        P("expert", "fsdp", None),
        P("expert", "fsdp", None),
        P(both, None),
        P(both, None),
        P(),
        P(both, None),
    )
    return jax.shard_map(
        on_device,
        mesh=mesh,
        in_specs=placed,
        out_specs=(
            P(both, None),
            P(both, None),
            P(both),
            P(both, None),
            P(both, None),
            P(both, None),
            P(both),
            P(both),
            P(both, None),
            P(both),
            P(both, None),
            P("expert", "fsdp", None),
            P("expert", "fsdp", None),
        ),
        check_vma=False,
    )
```

```python
import math

import jax
import jax.numpy as jnp
from jax import lax
from jax.experimental import pallas as pl
from jax.experimental.pallas import tpu as pltpu
from jax.sharding import PartitionSpec as P

HEAD = 128
EFF = 1024
TOPK = 8
PLANES = 4

epsilon = 1e-06
rope_base = 10000.0
masked = -1e30
bf16 = jnp.bfloat16
f32 = jnp.float32
score_scale = 1.0 / math.sqrt(HEAD)
VMEM_BYTES = 40 * 1024 * 1024


def swap(block, axis, mask):
    count = lax.axis_size(axis)
    return lax.ppermute(block, axis, [(i, i ^ mask) for i in range(count)])


def contract_rows(left, right, out=f32):
    return lax.dot_general(
        left, right, (((0,), (0,)), ((), ())), preferred_element_type=f32
    ).astype(out)


def contract_cols(left, right, out=f32):
    return lax.dot_general(
        left, right, (((1,), (1,)), ((), ())), preferred_element_type=f32
    ).astype(out)


def matmul(left, right):
    return jnp.dot(left, right, preferred_element_type=f32)


def rms_scale(values, gain):
    inverse = lax.rsqrt(jnp.mean(values * values, axis=-1, keepdims=True) + epsilon)
    return (values * inverse * gain, inverse)


def rms_back(values, inverse, gain, upstream):
    scaled = upstream * gain
    inner_sum = jnp.sum(scaled * values, axis=-1, keepdims=True)
    length_now = values.shape[-1]
    grad_values = inverse * scaled - values * (inverse * inverse * inverse) * (
        inner_sum / length_now
    )
    return (grad_values, upstream * values * inverse)


def rotary_tables(positions):
    half_width = HEAD // 2
    freq_steps = jnp.arange(half_width, dtype=f32)
    frequency = jnp.exp(freq_steps * (-2.0 * math.log(rope_base) / HEAD))
    angles = positions.astype(f32)[:, None] * frequency[None, :]
    cosine, sine = jnp.cos(angles), jnp.sin(angles)
    return jnp.stack(
        [
            jnp.concatenate([cosine, cosine], axis=-1),
            jnp.concatenate([-sine, sine], axis=-1),
        ]
    )


def unrope(upstream, cosine, sine):
    return upstream * cosine - pltpu.roll(upstream, HEAD // 2, 1) * sine


def normed_rope(values, gain, cosine, sine):
    normed, inverse = rms_scale(values, gain)
    turned = normed * cosine + pltpu.roll(normed, HEAD // 2, 1) * sine
    return turned.astype(bf16), inverse, normed


def attention_forward(query_raw, key_raw, value_low, tables, scales, live):
    queries, half = query_raw.shape
    span = key_raw.shape[0]
    heads = half // HEAD
    step = queries // 2

    def kernel(q_ref, k_ref, v_ref, table_ref, scale_ref, live_ref, out_ref, lse_ref):
        cosine, sine = table_ref[0], table_ref[1]
        key_low, _, _ = normed_rope(k_ref[...], scale_ref[1:2], cosine, sine)
        value_turned = v_ref[...].astype(f32).T.astype(bf16)
        live_now = jnp.concatenate([live_ref[...]] * (step // HEAD), axis=1) > 0.0
        for part in range(2):
            at = slice(part * step, (part + 1) * step)
            query_low, _, _ = normed_rope(q_ref[at], scale_ref[0:1], cosine[at], sine[at])
            scores = jnp.where(live_now, contract_cols(key_low, query_low), masked)
            peak = jnp.max(scores, axis=0, keepdims=True)
            exponent = jnp.exp((scores - peak) * score_scale)
            running = jnp.sum(exponent, axis=0, keepdims=True)
            turned = matmul(value_turned, exponent.astype(bf16)) / running
            out_ref[at] = turned.T.astype(bf16)
            lse_ref[0, :, at] = jnp.broadcast_to(
                peak * score_scale + jnp.log(running), (8, step)
            )

    column = lambda rows: pl.BlockSpec((rows, HEAD), lambda h: (0, h))
    return pl.pallas_call(
        kernel,
        grid=(heads,),
        in_specs=[
            column(queries),
            column(span),
            column(span),
            pl.BlockSpec((2, span, HEAD), lambda h: (0, 0, 0)),
            pl.BlockSpec((8, HEAD), lambda h: (0, 0)),
            pl.BlockSpec((span, HEAD), lambda h: (0, 0)),
        ],
        out_specs=[column(queries), pl.BlockSpec((1, 8, queries), lambda h: (h, 0, 0))],
        out_shape=[
            jax.ShapeDtypeStruct((queries, half), bf16),
            jax.ShapeDtypeStruct((heads, 8, queries), f32),
        ],
        compiler_params=pltpu.CompilerParams(vmem_limit_bytes=VMEM_BYTES),
        name="attention_forward",
    )(query_raw, key_raw, value_low, tables, scales, live)


def attention_backward(query_raw, key_raw, value_low, attended_grad, lse, tables, scales, live):
    queries, half = query_raw.shape
    span = key_raw.shape[0]
    heads = half // HEAD
    step = queries // 2

    def fold(terms):
        return jnp.sum(terms.reshape(-1, 8, HEAD), axis=0)

    def kernel(
        q_ref, k_ref, v_ref, grad_ref, lse_ref, table_ref, scale_ref, live_ref,
        dq_ref, dk_ref, dv_ref, gains_ref,
    ):
        cosine, sine = table_ref[0], table_ref[1]
        key_raw = k_ref[...]
        key_low, key_inverse, _ = normed_rope(key_raw, scale_ref[1:2], cosine, sine)
        key_turned = key_low.astype(f32).T.astype(bf16)
        live_now = jnp.concatenate([live_ref[...]] * (step // HEAD), axis=1) > 0.0
        key_grad = jnp.zeros((span, HEAD), f32)
        value_grad = jnp.zeros((span, HEAD), f32)
        query_gain = jnp.zeros((8, HEAD), f32)
        for part in range(2):
            at = slice(part * step, (part + 1) * step)
            query_raw = q_ref[at]
            query_low, query_inverse, _ = normed_rope(
                query_raw, scale_ref[0:1], cosine[at], sine[at]
            )
            upstream = grad_ref[at]
            scores = jnp.where(
                live_now, contract_cols(key_low, query_low) * score_scale, masked
            )
            probs = jnp.exp(scores - lse_ref[0, 0:1, at])
            probs_grad = contract_cols(v_ref[...], upstream)
            inner = jnp.sum(probs * probs_grad, axis=0, keepdims=True)
            score_grad = (probs * (probs_grad - inner)).astype(bf16)
            value_grad = value_grad + matmul(probs.astype(bf16), upstream)
            key_grad = key_grad + matmul(score_grad, query_low)
            query_grad = matmul(key_turned, score_grad).T * score_scale
            query_grad, terms = rms_back(
                query_raw,
                query_inverse,
                scale_ref[0:1],
                unrope(query_grad, cosine[at], sine[at]),
            )
            dq_ref[at] = query_grad.astype(bf16)
            query_gain = query_gain + fold(terms)
        dv_ref[...] = value_grad.astype(bf16)
        key_grad, terms = rms_back(
            key_raw, key_inverse, scale_ref[1:2], unrope(key_grad * score_scale, cosine, sine)
        )
        dk_ref[...] = key_grad.astype(bf16)
        gains = jnp.stack([query_gain, fold(terms)])

        @pl.when(pl.program_id(0) == 0)
        def _():
            gains_ref[...] = gains

        @pl.when(pl.program_id(0) > 0)
        def _():
            gains_ref[...] = gains_ref[...] + gains

    column = lambda rows: pl.BlockSpec((rows, HEAD), lambda h: (0, h))
    return pl.pallas_call(
        kernel,
        grid=(heads,),
        in_specs=[
            column(queries),
            column(span),
            column(span),
            column(queries),
            pl.BlockSpec((1, 8, queries), lambda h: (h, 0, 0)),
            pl.BlockSpec((2, span, HEAD), lambda h: (0, 0, 0)),
            pl.BlockSpec((8, HEAD), lambda h: (0, 0)),
            pl.BlockSpec((span, HEAD), lambda h: (0, 0)),
        ],
        out_specs=[
            column(queries),
            column(span),
            column(span),
            pl.BlockSpec((2, 8, HEAD), lambda h: (0, 0, 0)),
        ],
        out_shape=[
            jax.ShapeDtypeStruct((queries, half), bf16),
            jax.ShapeDtypeStruct((span, half), bf16),
            jax.ShapeDtypeStruct((span, half), bf16),
            jax.ShapeDtypeStruct((2, 8, HEAD), f32),
        ],
        compiler_params=pltpu.CompilerParams(vmem_limit_bytes=VMEM_BYTES),
        name="attention_backward",
    )(query_raw, key_raw, value_low, attended_grad, lse, tables, scales, live)


def in_order(flag, first, second, axis):
    return jnp.where(
        flag == 0,
        jnp.concatenate([first, second], axis=axis),
        jnp.concatenate([second, first], axis=axis),
    )


def pick(values, start, width, axis=1):
    return lax.dynamic_slice_in_dim(values, start, width, axis=axis)


def split_three(values):
    high = lax.reduce_precision(values, 8, 7)
    rest = values - high
    middle = lax.reduce_precision(rest, 8, 7)
    low = rest - middle
    return (high.astype(bf16), middle.astype(bf16), low.astype(bf16))


def on_device(
    hidden_in,
    prenorm_gain,
    query_weight,
    key_weight,
    value_weight,
    querynorm_gain,
    keynorm_gain,
    output_weight,
    postnorm_gain,
    router_weight,
    expert_inner,
    expert_outer,
    expert_ids,
    pair_order,
    sequence_lengths,
    cotangent,
):
    tokens, width = hidden_in.shape
    owners = lax.axis_size("expert")
    sharers = lax.axis_size("fsdp")
    devices = owners * sharers
    ring = owners // PLANES
    bits = ring.bit_length() - 1
    capacity = tokens * TOPK // owners
    half = width // 2
    owner = lax.axis_index("expert")
    core = lax.axis_index("fsdp")
    parity = owner % 2
    length = lax.dynamic_index_in_dim(sequence_lengths, owner // 2, 0, keepdims=False)

    plane = owner // ring

    def gather_owners(block):
        return lax.all_gather(block, "expert", axis=0, tiled=True)

    def bit_of(b):
        return (owner >> b) & 1

    def gather_planes(block):
        d1, d2, d3 = [swap(block, "expert", d * ring) for d in range(1, PLANES)]
        low, high = plane & 1, plane >> 1
        return in_order(high, in_order(low, block, d1, 0), in_order(low, d2, d3, 0), 0)

    def gather_plane(now, order):
        rows, columns = now.shape[0] // PLANES, now.shape[1]
        now = now.reshape((PLANES,) + (1,) * bits + (rows, columns))
        for b in order:
            now = in_order(bit_of(b), now, swap(now, "expert", 1 << b), bits - b)
        return now.reshape(owners * rows, columns)

    def split_columns(values, b):
        each = values.shape[1] // owners

        def side(bit):
            return jnp.concatenate(
                [
                    pick(values, ((k << (b + 1)) + (bit << b)) * each, each << b)
                    for k in range(owners >> (b + 1))
                ],
                axis=1,
            )

        return side(bit_of(b)), side(1 - bit_of(b))

    def scatter_rest(now, order):
        columns = now.shape[1]
        axes = [b for b in reversed(range(bits)) if b != order[0]]
        rows = width // owners
        for b in order[1:]:
            now = now.reshape([PLANES] + [2] * len(axes) + [rows, columns])
            at = 1 + axes.index(b)
            kept = lax.dynamic_index_in_dim(now, bit_of(b), at, keepdims=False)
            sent = lax.dynamic_index_in_dim(now, 1 - bit_of(b), at, keepdims=False)
            axes.remove(b)
            now = kept + swap(sent.astype(bf16), "expert", 1 << b).astype(f32)
        return now.reshape(PLANES, rows, columns)

    def scatter_planes(now):
        total = lax.dynamic_index_in_dim(now, plane, 0, keepdims=False)
        for d in range(1, PLANES):
            sent = lax.dynamic_index_in_dim(now, plane ^ d, 0, keepdims=False)
            total = total + swap(sent.astype(bf16), "expert", d * ring).astype(f32)
        return total

    descending = list(range(bits))[::-1]
    ascending = list(range(bits))

    rows_dev = width // devices
    small = jnp.concatenate(
        [
            prenorm_gain,
            postnorm_gain,
            querynorm_gain,
            keynorm_gain,
            router_weight.reshape(-1),
        ]
    )
    cut = [0]
    for piece in (prenorm_gain, postnorm_gain, querynorm_gain, keynorm_gain, router_weight):
        cut.append(cut[-1] + piece.size)
    lanes = 128
    small_rows = -(-cut[-1] // (lanes * 16)) * 16
    small = jnp.pad(small, (0, small_rows * lanes - cut[-1])).reshape(small_rows, lanes)
    other_chip = swap(hidden_in, "expert", 1)
    hidden_own_peer = swap(hidden_in, "fsdp", 1)
    hidden_other_peer = swap(other_chip, "fsdp", 1)
    hidden_seq = jnp.concatenate(
        [hidden_in, hidden_own_peer, other_chip, hidden_other_peer], axis=0
    )

    stacked = jnp.stack([query_weight, key_weight, value_weight, output_weight])
    mine = pick(stacked, core * half, half, axis=2)
    theirs = swap(pick(stacked, (1 - core) * half, half, axis=2), "fsdp", 1)
    shards = in_order(core, mine, theirs, 1)
    query_own = gather_owners(shards[0])
    output_own = gather_owners(shards[3])
    small_pair = in_order(core, small, swap(small, "fsdp", 1), 0).reshape(-1, half)
    small_tall = -(-small_pair.shape[0] // 16) * 16
    small_pair = jnp.pad(small_pair, ((0, small_tall - small_pair.shape[0]), (0, 0)))
    key_tall = shards.shape[1] + small_tall
    firsts = gather_planes(jnp.concatenate([shards[1], small_pair, shards[2]], axis=0))
    firsts = firsts.reshape(PLANES, key_tall + shards.shape[1], half)

    inner_now = lax.all_gather(expert_inner, "fsdp", axis=1, tiled=True)[0]
    outer_now = lax.all_gather(expert_outer, "fsdp", axis=1, tiled=True)[0]
    extra_width = -(-3 * owners // 128) * 128
    inner_pad = jnp.pad(inner_now, ((0, extra_width), (0, 0)))

    span = 2 * sharers * tokens
    local = jnp.arange(tokens, dtype=jnp.int32)
    positions = jnp.concatenate(
        [
            ((parity ^ a) * sharers + (core ^ c)) * tokens + local
            for a in range(2)
            for c in range(2)
        ]
    )
    token_live = positions[:tokens] < length
    key_live = positions < length
    tables = rotary_tables(positions)
    live_lanes = jnp.broadcast_to(key_live.astype(f32)[:, None], (span, HEAD))
    expert_range = jnp.arange(owners, dtype=jnp.int32)
    hot = expert_ids[:, :, None] == expert_range[None, None, :]
    chosen = jnp.any(hot, axis=1)
    far = jnp.int32(1 << 30)
    order_of = jnp.sum(
        jnp.where(hot, pair_order.reshape(tokens, TOPK)[:, :, None], 0), axis=1
    )
    order_of = jnp.where(chosen & token_live[:, None], order_of, far)
    by_expert = order_of.T
    rank_of = jnp.sum(
        (by_expert[:, None, :] < by_expert[:, :, None]).astype(jnp.int32), axis=-1
    ).T
    rank_of = jnp.where(order_of == far, capacity, jnp.minimum(rank_of, capacity))
    kept = (rank_of < capacity).astype(f32)

    def widened(main, extra):
        pad = -extra.shape[1] % 128
        return jnp.concatenate([main, jnp.pad(extra, ((0, 0), (0, pad)))], axis=1)

    upstream_low = jnp.where(token_live[:, None], cotangent, jnp.zeros((), bf16))
    upstream = upstream_low.astype(f32)
    select = (expert_range[:, None] == (owner ^ jnp.arange(ring))[None, :]).astype(bf16)

    last = PLANES - 1

    def planes_of(block):
        return [block] + [swap(block, "expert", d * ring) for d in range(1, PLANES)]

    def exchange(rows):
        return [rows[:capacity]] + [
            swap(rows[j * capacity : (j + 1) * capacity], "expert", j) for j in range(1, ring)
        ]

    up_wide = widened(upstream_low, rank_of.astype(bf16))
    up_wide, firsts = lax.optimization_barrier((up_wide, firsts))
    key_all = gather_plane(firsts[:, :key_tall].reshape(-1, half), descending)
    value_own = gather_plane(firsts[:, key_tall:].reshape(-1, half), ascending)
    key_all = key_all.reshape(owners, key_tall, half)
    key_own = key_all[:, : shards.shape[1]].reshape(width, half)
    small_all = key_all[:, shards.shape[1] :].reshape(owners, small_tall * half)
    small_all = small_all[:, : sharers * small_rows * lanes].reshape(devices, -1)
    first_gain = small_all[:, cut[0] : cut[1]].reshape(width).astype(f32)
    second_gain = small_all[:, cut[1] : cut[2]].reshape(width).astype(f32)
    query_scale = small_all[:, cut[2] : cut[3]].reshape(HEAD).astype(f32)
    key_scale = small_all[:, cut[3] : cut[4]].reshape(HEAD).astype(f32)
    router_full = small_all[:, cut[4] : cut[5]].reshape(width, owners)

    output_peer = swap(output_own, "fsdp", 1)
    up_planes = planes_of(up_wide)
    up_planes, key_late, value_late = lax.optimization_barrier((up_planes, key_own, value_own))

    def exchange_all(blocks):
        got = [blocks]
        for j in range(1, ring):
            at = slice(j * capacity, (j + 1) * capacity)
            sent = jnp.concatenate([block[at] for block in blocks], axis=0)
            got.append(swap(sent, "expert", j))
        return [
            [blocks[d][:capacity]]
            + [got[j][d * capacity : (d + 1) * capacity] for j in range(1, ring)]
            for d in range(len(blocks))
        ]

    pickers, up_picked = [], []
    for d in range(PLANES):
        rank_rel = matmul(up_planes[d][:, width : width + owners], select)
        hits = rank_rel[:, :, None] == jnp.arange(capacity, dtype=f32)[None, None, :]
        picker = hits.astype(bf16).reshape(tokens, ring * capacity)
        pickers.append(picker)
        up_picked.append(contract_rows(picker, up_planes[d][:, :width], bf16))
    up_arrived = exchange_all(up_picked)

    scales = jnp.pad(jnp.stack([query_scale, key_scale]), ((0, 6), (0, 0)))
    hidden_f = hidden_seq.astype(f32)
    first_normed, first_inverse = rms_scale(hidden_f, first_gain)
    first_low = first_normed.astype(bf16)
    key_raw = matmul(first_low, key_own)
    value_low = matmul(first_low, value_own).astype(bf16)
    query_raw = matmul(first_low[: 2 * tokens], query_own)
    attended, lse = attention_forward(
        query_raw, key_raw, value_low, tables, scales, live_lanes
    )
    left_x = split_columns(first_low, 0)
    left_y = split_columns(first_low, bits - 1)
    attended_cross = swap(attended[tokens:], "fsdp", 1)
    attended_full = in_order(core, attended[:tokens], attended_cross, 1)
    attended_peer = swap(attended_full, "fsdp", 1)
    branch = in_order(
        core, matmul(attended_full, output_own), matmul(attended_full, output_peer), 1
    )
    residual = hidden_in.astype(f32) + branch
    second_normed, second_inverse = rms_scale(residual, second_gain)
    mixed_in = second_normed.astype(bf16)
    logits = matmul(mixed_in, router_full)
    shown = jnp.where(chosen, logits, masked)
    gate_exp = jnp.where(chosen, jnp.exp(shown - jnp.max(shown, axis=-1, keepdims=True)), 0.0)
    gate_soft = gate_exp / jnp.sum(gate_exp, axis=-1, keepdims=True)

    extra = jnp.concatenate(split_three(gate_soft * kept), axis=1)
    in_planes = planes_of(widened(mixed_in, extra))
    up_arrived, mixed_late = lax.optimization_barrier((up_arrived, mixed_in))
    up_rows = jnp.concatenate([p for parts in up_arrived for p in parts], axis=0)
    picked = [contract_rows(pickers[d], in_planes[d], bf16) for d in range(PLANES)]
    picked[0], up_rows = lax.optimization_barrier((picked[0], up_rows))
    column = jnp.arange(extra_width, dtype=jnp.int32)[None, :]
    own_column = (column % owners == owner) & (column < 3 * owners)
    plane_rows = ring * capacity

    hidden_up = contract_cols(up_rows, outer_now)
    row_inputs, hidden_gated, both_grad, rows_back, rows_out = [], [], [], [], []
    out_arrived = [None] * PLANES
    for d in range(PLANES):
        rows = exchange(picked[d])
        if d < last:
            rows, picked[d + 1] = lax.optimization_barrier((rows, picked[d + 1]))
        if d == 0:
            rows, left_x, left_y, attended_peer = lax.optimization_barrier(
                (rows, left_x, left_y, attended_peer)
            )
        elif d == 1 or d == last:
            early = 0 if d == 1 else 1
            out_rows, rows = lax.optimization_barrier((rows_out[early], rows))
            out_arrived[early] = exchange(out_rows)
        rows = jnp.concatenate(rows, axis=0)
        if d:
            rows, rows_back[-1] = lax.optimization_barrier((rows, rows_back[-1]))
        marks = rows[:, width:].astype(f32)
        row_gate = jnp.sum(jnp.where(own_column, marks, 0.0), axis=1, keepdims=True)
        gate_up = matmul(rows, inner_pad)
        up_back = hidden_up[d * plane_rows : (d + 1) * plane_rows]
        gate_part = gate_up[:, :EFF]
        up_part = gate_up[:, EFF:]
        gate_sigmoid = jax.nn.sigmoid(gate_part)
        activated = gate_part * gate_sigmoid
        hidden_rows = activated * up_part
        gated = (hidden_rows * row_gate).astype(bf16)
        row_gate_grad = jnp.sum(hidden_rows * up_back, axis=1, keepdims=True)
        hidden_grad = up_back * row_gate
        grads = jnp.concatenate(
            [
                hidden_grad * up_part * gate_sigmoid * (1.0 + gate_part * (1.0 - gate_sigmoid)),
                hidden_grad * activated,
            ],
            axis=-1,
        ).astype(bf16)
        part_of = jnp.concatenate(
            [jnp.broadcast_to(p, (p.shape[0], owners)) for p in split_three(row_gate_grad)],
            axis=1,
        )
        part_of = jnp.pad(part_of, ((0, 0), (0, extra_width - 3 * owners)))
        part_of = jnp.where(own_column, part_of, jnp.zeros((), bf16))
        rows_back.append(
            contract_cols(grads, inner_pad, bf16) + jnp.pad(part_of, ((0, 0), (width, 0)))
        )
        rows_out.append(matmul(gated, outer_now).astype(bf16))
        row_inputs.append(rows[:, :width])
        hidden_gated.append(gated)
        both_grad.append(grads)
    arrived = [None] * PLANES
    for d in reversed(range(PLANES)):
        block = rows_back[d]
        if d < last:
            block, arrived[d + 1] = lax.optimization_barrier((block, arrived[d + 1]))
        else:
            block, out_arrived[:2] = lax.optimization_barrier((block, out_arrived[:2]))
        arrived[d] = exchange(block)
    arrived[last], row_inputs, hidden_gated, both_grad = lax.optimization_barrier(
        (arrived[last], row_inputs, hidden_gated, both_grad)
    )
    row_inputs = jnp.concatenate(row_inputs, axis=0)
    hidden_gated = jnp.concatenate(hidden_gated, axis=0)
    both_grad = jnp.concatenate(both_grad, axis=0)

    def at_planes(arrived):
        came = [None] * PLANES
        for d in reversed(range(PLANES)):
            part = matmul(pickers[d], jnp.concatenate(arrived[d], axis=0))
            came[d] = swap(part.astype(bf16), "expert", d * ring) if d else part
        return came

    def added(came):
        total = came[0]
        for part in came[1:]:
            total = total + part.astype(f32)
        return total

    eff_half = EFF // 2
    inner_sent = contract_rows(pick(row_inputs, (1 - core) * half, half), both_grad, bf16)
    inner_kept = contract_rows(pick(row_inputs, core * half, half), both_grad)
    outer_sent = contract_rows(
        pick(hidden_gated, (1 - core) * eff_half, eff_half), up_rows, bf16
    )
    outer_kept = contract_rows(pick(hidden_gated, core * eff_half, eff_half), up_rows)
    back = added(at_planes(arrived))
    back, late_out, inner_sent, inner_kept, outer_sent, outer_kept = lax.optimization_barrier(
        (back, rows_out[2:], inner_sent, inner_kept, outer_sent, outer_kept)
    )
    inner_grad = inner_kept + swap(inner_sent, "fsdp", 1).astype(f32)
    outer_grad = outer_kept + swap(outer_sent, "fsdp", 1).astype(f32)
    out_arrived[2:] = exchange_all(late_out)
    mixed_grad = back[:, :width]
    gate_grad = (
        back[:, width : width + owners]
        + back[:, width + owners : width + 2 * owners]
        + back[:, width + 2 * owners : width + 3 * owners]
    )

    soft_grad = gate_soft * (gate_grad - jnp.sum(gate_soft * gate_grad, axis=-1, keepdims=True))
    logit_grad = soft_grad.astype(bf16)
    router_local = contract_rows(mixed_late, logit_grad)
    mixed_grad = mixed_grad + contract_cols(logit_grad, router_full)
    residual_part, second_terms = rms_back(residual, second_inverse, second_gain, mixed_grad)
    residual_grad = upstream + residual_part
    branch_low = residual_grad.astype(bf16)
    branch_mine = pick(branch_low, core * half, half)
    branch_theirs = pick(branch_low, (1 - core) * half, half)
    attended_grad = (
        contract_cols(branch_mine, output_own) + contract_cols(branch_theirs, output_peer)
    ).astype(bf16)
    grad_mine = pick(attended_grad, core * half, half)
    grad_cross = swap(pick(attended_grad, (1 - core) * half, half), "fsdp", 1)
    attended_grad = jnp.concatenate([grad_mine, grad_cross], axis=0)

    attended_both = jnp.concatenate([attended_full, attended_peer], axis=0)
    branch_both = jnp.concatenate([branch_mine, swap(branch_theirs, "fsdp", 1)], axis=0)
    output_local = contract_rows(attended_both, branch_both, bf16)

    attended_grad, output_local = lax.optimization_barrier((attended_grad, output_local))
    output_block = lax.psum_scatter(output_local, "expert", scatter_dimension=0, tiled=True)
    output_block = output_block.astype(f32)
    query_low_grad, key_low_grad, value_low_grad, gain_terms = attention_backward(
        query_raw, key_raw, value_low, attended_grad, lse, tables, scales, live_lanes
    )

    out_arrived, query_low_grad, key_low_grad, value_low_grad = lax.optimization_barrier(
        (out_arrived, query_low_grad, key_low_grad, value_low_grad)
    )
    quarter = half // 2
    chip = 2 * tokens
    y_bit = bits - 1

    value_sent = contract_rows(left_y[1], value_low_grad, bf16)
    key_sent = contract_rows(left_x[1], key_low_grad, bf16)
    value_sent, key_sent, query_late, key_grad_late, value_grad_late = lax.optimization_barrier(
        (value_sent, key_sent, query_low_grad, key_low_grad, value_low_grad)
    )
    value_came = swap(value_sent, "expert", 1 << y_bit)
    key_came = swap(key_sent, "expert", 1)
    out_came = at_planes(out_arrived)
    query_sent = [
        contract_rows(left_x[1][:chip], query_late[:, :quarter], bf16),
        contract_rows(left_y[1][:chip], query_late[:, quarter:], bf16),
    ]
    value_kept = contract_rows(left_y[0], value_grad_late)
    key_kept = contract_rows(left_x[0], key_grad_late)
    kept = [
        contract_rows(left_x[0][:chip], query_late[:, :quarter]),
        contract_rows(left_y[0][:chip], query_late[:, quarter:]),
    ]
    kv_grad = contract_cols(key_grad_late, key_late) + contract_cols(value_grad_late, value_late)
    q_grad = contract_cols(query_late, query_own)
    own_part = kv_grad[:tokens] + q_grad[:tokens]
    peer_part = kv_grad[tokens : 2 * tokens] + q_grad[tokens:]
    far_part = kv_grad[2 * tokens : 3 * tokens]
    far_peer = kv_grad[3 * tokens :]
    crossed = swap(jnp.concatenate([peer_part, far_peer], axis=0).astype(bf16), "fsdp", 1)
    own_part = own_part + crossed[:tokens].astype(f32)
    far_part = (far_part + crossed[tokens:].astype(f32)).astype(bf16)
    value_came, key_came, out_came, query_sent, value_kept, key_kept, kept, far_part = (
        lax.optimization_barrier(
            (value_came, key_came, out_came, query_sent, value_kept, key_kept, kept, far_part)
        )
    )

    query_came = [swap(query_sent[0], "expert", 1), swap(query_sent[1], "expert", 1 << y_bit)]
    value_now = scatter_rest(value_kept + value_came.astype(f32), descending)
    key_now = scatter_rest(key_kept + key_came.astype(f32), ascending)
    far_back = swap(far_part, "expert", 1)
    query_came, value_now, key_now, far_back = lax.optimization_barrier(
        (query_came, value_now, key_now, far_back)
    )

    query_now = [
        scatter_rest(kept[0] + query_came[0].astype(f32), ascending),
        scatter_rest(kept[1] + query_came[1].astype(f32), descending),
    ]
    pair_block = scatter_planes(jnp.concatenate([value_now, key_now], axis=2))
    query_now, pair_block = lax.optimization_barrier((query_now, pair_block))

    query_block = scatter_planes(jnp.concatenate(query_now, axis=2))
    value_block, key_block = pair_block[:, :half], pair_block[:, half:]
    layer_out = (residual + added(out_came)).astype(bf16)

    normed_grad = own_part + far_back.astype(f32)
    hidden_part, first_terms = rms_back(
        hidden_f[:tokens], first_inverse[:tokens], first_gain, normed_grad
    )
    input_grad = residual_grad + hidden_part

    small_grads = jnp.concatenate(
        [
            jnp.sum(first_terms, axis=0).reshape(devices, -1),
            jnp.sum(second_terms, axis=0).reshape(devices, -1),
            jnp.sum(gain_terms[0], axis=0).reshape(devices, -1),
            jnp.sum(gain_terms[1], axis=0).reshape(devices, -1),
            router_local.reshape(devices, -1),
        ],
        axis=1,
    )
    small_grads = jnp.pad(small_grads, ((0, 0), (0, small_rows * lanes - cut[-1])))
    now = small_grads.reshape([PLANES] + [2] * bits + [2, small_rows, lanes])
    at = bits + 1
    sent = lax.dynamic_index_in_dim(now, 1 - core, at, keepdims=False)
    now = lax.dynamic_index_in_dim(now, core, at, keepdims=False) + swap(sent, "fsdp", 1)
    for b in range(bits):
        at = bits - b
        sent = lax.dynamic_index_in_dim(now, 1 - bit_of(b), at, keepdims=False)
        now = lax.dynamic_index_in_dim(now, bit_of(b), at, keepdims=False) + swap(
            sent, "expert", 1 << b
        )
    small_sum = lax.dynamic_index_in_dim(now, plane, 0, keepdims=False)
    for d in range(1, PLANES):
        sent = lax.dynamic_index_in_dim(now, plane ^ d, 0, keepdims=False)
        small_sum = small_sum + swap(sent, "expert", d * ring)
    small_sum = small_sum.reshape(-1)

    def whole_rows(block):
        keep = pick(block, core * rows_dev, rows_dev, 0)
        cross = swap(pick(block, (1 - core) * rows_dev, rows_dev, 0), "fsdp", 1)
        return in_order(core, keep, cross, 1)

    weight_grads = [whole_rows(b) for b in (query_block, key_block, value_block, output_block)]
    return (
        layer_out,
        input_grad,
        small_sum[cut[0] : cut[1]],
        weight_grads[0],
        weight_grads[1],
        weight_grads[2],
        small_sum[cut[2] : cut[3]],
        small_sum[cut[3] : cut[4]],
        weight_grads[3],
        small_sum[cut[1] : cut[2]],
        small_sum[cut[4] : cut[5]].reshape(rows_dev, owners),
        inner_grad[None],
        outer_grad[None],
    )


def solution(mesh):
    both = ("expert", "fsdp")
    placed = (
        P(both, None),
        P(both),
        P(both, None),
        P(both, None),
        P(both, None),
        P(both),
        P(both),
        P(both, None),
        P(both),
        P(both, None),
        P("expert", "fsdp", None),
        P("expert", "fsdp", None),
        P(both, None),
        P(both, None),
        P(),
        P(both, None),
    )
    return jax.shard_map(
        on_device,
        mesh=mesh,
        in_specs=placed,
        out_specs=(
            P(both, None),
            P(both, None),
            P(both),
            P(both, None),
            P(both, None),
            P(both, None),
            P(both),
            P(both),
            P(both, None),
            P(both),
            P(both, None),
            P("expert", "fsdp", None),
            P("expert", "fsdp", None),
        ),
        check_vma=False,
    )
```

```python
import math

import jax
import jax.numpy as jnp
from jax import lax
from jax.experimental import pallas as pl
from jax.experimental.pallas import tpu as pltpu
from jax.sharding import PartitionSpec as P

HEAD = 128
EFF = 1024
TOPK = 8
PLANES = 4

epsilon = 1e-06
rope_base = 10000.0
masked = -1e30
bf16 = jnp.bfloat16
f32 = jnp.float32
score_scale = 1.0 / math.sqrt(HEAD)
VMEM_BYTES = 40 * 1024 * 1024


def swap(block, axis, mask):
    count = lax.axis_size(axis)
    return lax.ppermute(block, axis, [(i, i ^ mask) for i in range(count)])


def contract_rows(left, right, out=f32):
    return lax.dot_general(
        left, right, (((0,), (0,)), ((), ())), preferred_element_type=f32
    ).astype(out)


def contract_cols(left, right, out=f32):
    return lax.dot_general(
        left, right, (((1,), (1,)), ((), ())), preferred_element_type=f32
    ).astype(out)


def matmul(left, right):
    return jnp.dot(left, right, preferred_element_type=f32)


def rms_scale(values, gain):
    inverse = lax.rsqrt(jnp.mean(values * values, axis=-1, keepdims=True) + epsilon)
    return (values * inverse * gain, inverse)


def rms_back(values, inverse, gain, upstream):
    scaled = upstream * gain
    inner_sum = jnp.sum(scaled * values, axis=-1, keepdims=True)
    length_now = values.shape[-1]
    grad_values = inverse * scaled - values * (inverse * inverse * inverse) * (
        inner_sum / length_now
    )
    return (grad_values, upstream * values * inverse)


def rotary_tables(positions):
    half_width = HEAD // 2
    freq_steps = jnp.arange(half_width, dtype=f32)
    frequency = jnp.exp(freq_steps * (-2.0 * math.log(rope_base) / HEAD))
    angles = positions.astype(f32)[:, None] * frequency[None, :]
    cosine, sine = jnp.cos(angles), jnp.sin(angles)
    return jnp.stack(
        [
            jnp.concatenate([cosine, cosine], axis=-1),
            jnp.concatenate([-sine, sine], axis=-1),
        ]
    )


def unrope(upstream, cosine, sine):
    return upstream * cosine - pltpu.roll(upstream, HEAD // 2, 1) * sine


def normed_rope(values, gain, cosine, sine):
    normed, inverse = rms_scale(values, gain)
    turned = normed * cosine + pltpu.roll(normed, HEAD // 2, 1) * sine
    return turned.astype(bf16), inverse, normed


def attention_forward(query_raw, key_raw, value_low, tables, scales, live):
    queries, half = query_raw.shape
    span = key_raw.shape[0]
    heads = half // HEAD
    step = min(queries, 256)

    def kernel(q_ref, k_ref, v_ref, table_ref, scale_ref, live_ref, out_ref, lse_ref):
        cosine, sine = table_ref[0], table_ref[1]
        key_low, _, _ = normed_rope(k_ref[...], scale_ref[1:2], cosine, sine)
        value_turned = v_ref[...].astype(f32).T.astype(bf16)
        live_now = jnp.concatenate([live_ref[...]] * (step // HEAD), axis=1) > 0.0
        for part in range(queries // step):
            at = slice(part * step, (part + 1) * step)
            query_low, _, _ = normed_rope(q_ref[at], scale_ref[0:1], cosine[at], sine[at])
            scores = jnp.where(live_now, contract_cols(key_low, query_low), masked)
            peak = jnp.max(scores, axis=0, keepdims=True)
            exponent = jnp.exp((scores - peak) * score_scale)
            running = jnp.sum(exponent, axis=0, keepdims=True)
            turned = matmul(value_turned, exponent.astype(bf16)) / running
            out_ref[at] = turned.T.astype(bf16)
            lse_ref[0, :, at] = jnp.broadcast_to(
                peak * score_scale + jnp.log(running), (8, step)
            )

    column = lambda rows: pl.BlockSpec((rows, HEAD), lambda h: (0, h))
    return pl.pallas_call(
        kernel,
        grid=(heads,),
        in_specs=[
            column(queries),
            column(span),
            column(span),
            pl.BlockSpec((2, span, HEAD), lambda h: (0, 0, 0)),
            pl.BlockSpec((8, HEAD), lambda h: (0, 0)),
            pl.BlockSpec((span, HEAD), lambda h: (0, 0)),
        ],
        out_specs=[column(queries), pl.BlockSpec((1, 8, queries), lambda h: (h, 0, 0))],
        out_shape=[
            jax.ShapeDtypeStruct((queries, half), bf16),
            jax.ShapeDtypeStruct((heads, 8, queries), f32),
        ],
        compiler_params=pltpu.CompilerParams(vmem_limit_bytes=VMEM_BYTES),
        name="attention_forward",
    )(query_raw, key_raw, value_low, tables, scales, live)


def attention_backward(query_raw, key_raw, value_low, attended_grad, lse, tables, scales, live):
    queries, half = query_raw.shape
    span = key_raw.shape[0]
    heads = half // HEAD
    step = min(queries, 256)

    def fold(terms):
        return jnp.sum(terms.reshape(-1, 8, HEAD), axis=0)

    def kernel(
        q_ref, k_ref, v_ref, grad_ref, lse_ref, table_ref, scale_ref, live_ref,
        dq_ref, dk_ref, dv_ref, gains_ref,
    ):
        cosine, sine = table_ref[0], table_ref[1]
        key_raw = k_ref[...]
        key_low, key_inverse, _ = normed_rope(key_raw, scale_ref[1:2], cosine, sine)
        key_turned = key_low.astype(f32).T.astype(bf16)
        live_now = jnp.concatenate([live_ref[...]] * (step // HEAD), axis=1) > 0.0
        key_grad = jnp.zeros((span, HEAD), f32)
        value_grad = jnp.zeros((span, HEAD), f32)
        query_gain = jnp.zeros((8, HEAD), f32)
        for part in range(queries // step):
            at = slice(part * step, (part + 1) * step)
            query_raw = q_ref[at]
            query_low, query_inverse, _ = normed_rope(
                query_raw, scale_ref[0:1], cosine[at], sine[at]
            )
            upstream = grad_ref[at]
            scores = jnp.where(
                live_now, contract_cols(key_low, query_low) * score_scale, masked
            )
            probs = jnp.exp(scores - lse_ref[0, 0:1, at])
            probs_grad = contract_cols(v_ref[...], upstream)
            inner = jnp.sum(probs * probs_grad, axis=0, keepdims=True)
            score_grad = (probs * (probs_grad - inner)).astype(bf16)
            value_grad = value_grad + matmul(probs.astype(bf16), upstream)
            key_grad = key_grad + matmul(score_grad, query_low)
            query_grad = matmul(key_turned, score_grad).T * score_scale
            query_grad, terms = rms_back(
                query_raw,
                query_inverse,
                scale_ref[0:1],
                unrope(query_grad, cosine[at], sine[at]),
            )
            dq_ref[at] = query_grad.astype(bf16)
            query_gain = query_gain + fold(terms)
        dv_ref[...] = value_grad.astype(bf16)
        key_grad, terms = rms_back(
            key_raw, key_inverse, scale_ref[1:2], unrope(key_grad * score_scale, cosine, sine)
        )
        dk_ref[...] = key_grad.astype(bf16)
        gains = jnp.stack([query_gain, fold(terms)])

        @pl.when(pl.program_id(0) == 0)
        def _():
            gains_ref[...] = gains

        @pl.when(pl.program_id(0) > 0)
        def _():
            gains_ref[...] = gains_ref[...] + gains

    column = lambda rows: pl.BlockSpec((rows, HEAD), lambda h: (0, h))
    return pl.pallas_call(
        kernel,
        grid=(heads,),
        in_specs=[
            column(queries),
            column(span),
            column(span),
            column(queries),
            pl.BlockSpec((1, 8, queries), lambda h: (h, 0, 0)),
            pl.BlockSpec((2, span, HEAD), lambda h: (0, 0, 0)),
            pl.BlockSpec((8, HEAD), lambda h: (0, 0)),
            pl.BlockSpec((span, HEAD), lambda h: (0, 0)),
        ],
        out_specs=[
            column(queries),
            column(span),
            column(span),
            pl.BlockSpec((2, 8, HEAD), lambda h: (0, 0, 0)),
        ],
        out_shape=[
            jax.ShapeDtypeStruct((queries, half), bf16),
            jax.ShapeDtypeStruct((span, half), bf16),
            jax.ShapeDtypeStruct((span, half), bf16),
            jax.ShapeDtypeStruct((2, 8, HEAD), f32),
        ],
        compiler_params=pltpu.CompilerParams(vmem_limit_bytes=VMEM_BYTES),
        name="attention_backward",
    )(query_raw, key_raw, value_low, attended_grad, lse, tables, scales, live)


def in_order(flag, first, second, axis):
    return jnp.where(
        flag == 0,
        jnp.concatenate([first, second], axis=axis),
        jnp.concatenate([second, first], axis=axis),
    )


def pick(values, start, width, axis=1):
    return lax.dynamic_slice_in_dim(values, start, width, axis=axis)


def split_three(values):
    high = lax.reduce_precision(values, 8, 7)
    rest = values - high
    middle = lax.reduce_precision(rest, 8, 7)
    low = rest - middle
    return (high.astype(bf16), middle.astype(bf16), low.astype(bf16))


def on_device(
    hidden_in,
    prenorm_gain,
    query_weight,
    key_weight,
    value_weight,
    querynorm_gain,
    keynorm_gain,
    output_weight,
    postnorm_gain,
    router_weight,
    expert_inner,
    expert_outer,
    expert_ids,
    pair_order,
    sequence_lengths,
    cotangent,
):
    tokens, width = hidden_in.shape
    owners = lax.axis_size("expert")
    sharers = lax.axis_size("fsdp")
    devices = owners * sharers
    ring = owners // PLANES
    bits = ring.bit_length() - 1
    capacity = tokens * TOPK // owners
    half = width // 2
    quarter = width // 4
    pair_rows = 2 * width // owners
    owner = lax.axis_index("expert")
    core = lax.axis_index("fsdp")
    parity = owner % 2
    length = lax.dynamic_index_in_dim(sequence_lengths, owner // 2, 0, keepdims=False)

    plane = owner // ring

    def gather_owners(block):
        return lax.all_gather(block, "expert", axis=0, tiled=True)

    def bit_of(b):
        return (owner >> b) & 1

    def gather_planes(block):
        d1, d2, d3 = [swap(block, "expert", d * ring) for d in range(1, PLANES)]
        low, high = plane & 1, plane >> 1
        return in_order(high, in_order(low, block, d1, 0), in_order(low, d2, d3, 0), 0)

    def gather_plane(now, order):
        rows, columns = now.shape[0] // PLANES, now.shape[1]
        now = now.reshape((PLANES,) + (1,) * len(order) + (rows, columns))
        for b in order:
            now = in_order(bit_of(b), now, swap(now, "expert", 1 << b), bits - b)
        return now.reshape(-1, columns)

    def split_columns(values, b):
        each = values.shape[1] // owners

        def side(bit):
            return jnp.concatenate(
                [
                    pick(values, ((k << (b + 1)) + (bit << b)) * each, each << b)
                    for k in range(owners >> (b + 1))
                ],
                axis=1,
            )

        return side(bit_of(b)), side(1 - bit_of(b))

    def scatter_rest(now, order):
        columns = now.shape[1]
        axes = sorted(order[1:], reverse=True)
        for b in order[1:]:
            now = now.reshape([PLANES] + [2] * len(axes) + [-1, columns])
            at = 1 + axes.index(b)
            kept = lax.dynamic_index_in_dim(now, bit_of(b), at, keepdims=False)
            sent = lax.dynamic_index_in_dim(now, 1 - bit_of(b), at, keepdims=False)
            axes.remove(b)
            now = kept + swap(sent.astype(bf16), "expert", 1 << b).astype(f32)
        return now.reshape(PLANES, -1, columns)

    def scatter_planes(now):
        total = lax.dynamic_index_in_dim(now, plane, 0, keepdims=False)
        for d in range(1, PLANES):
            sent = lax.dynamic_index_in_dim(now, plane ^ d, 0, keepdims=False)
            total = total + swap(sent.astype(bf16), "expert", d * ring).astype(f32)
        return total

    descending = list(range(bits))[::-1]
    ascending = list(range(bits))

    def step_up(block, planes):
        return lax.ppermute(
            block, "expert", [(p * ring + i, (p + 1) * ring + i) for p in planes for i in range(ring)]
        )

    def step_down(block, planes):
        return lax.ppermute(
            block, "expert", [(p * ring + i, (p - 1) * ring + i) for p in planes for i in range(ring)]
        )

    rows_dev = width // devices
    small = jnp.concatenate(
        [
            prenorm_gain,
            postnorm_gain,
            querynorm_gain,
            keynorm_gain,
            router_weight.reshape(-1),
        ]
    )
    cut = [0]
    for piece in (prenorm_gain, postnorm_gain, querynorm_gain, keynorm_gain, router_weight):
        cut.append(cut[-1] + piece.size)
    lanes = 128
    small_rows = -(-cut[-1] // (lanes * 16)) * 16
    small = jnp.pad(small, (0, small_rows * lanes - cut[-1])).reshape(small_rows, lanes)
    small_two = in_order(parity, small, swap(small, "expert", 1), 0).reshape(2, 1, -1)
    small_four = in_order(core, small_two, swap(small_two, "fsdp", 1), 1).reshape(-1, quarter)
    small_tall = -(-small_four.shape[0] // 16) * 16
    small_four = jnp.pad(small_four, ((0, small_tall - small_four.shape[0]), (0, 0)))
    other_chip = swap(hidden_in, "expert", 1)
    hidden_own_peer = swap(hidden_in, "fsdp", 1)
    hidden_other_peer = swap(other_chip, "fsdp", 1)
    hidden_seq = jnp.concatenate(
        [hidden_in, hidden_own_peer, other_chip, hidden_other_peer], axis=0
    )

    stacked = jnp.stack([key_weight, value_weight, query_weight])
    mine = pick(stacked, parity * half, half, axis=2)
    theirs = swap(pick(stacked, (1 - parity) * half, half, axis=2), "expert", 1)
    shards = in_order(parity, mine, theirs, 1)
    mine = pick(shards, core * quarter, quarter, axis=2).reshape(3, 2, 1, -1, quarter)
    theirs = swap(pick(shards, (1 - core) * quarter, quarter, axis=2), "fsdp", 1)
    shards = in_order(core, mine, theirs.reshape(mine.shape), 2).reshape(3, pair_rows, quarter)
    key_first = gather_planes(jnp.concatenate([shards[0], small_four], axis=0))
    value_first = gather_planes(shards[1])
    query_first = gather_planes(shards[2])
    mine = pick(output_weight, core * half, half)
    theirs = swap(pick(output_weight, (1 - core) * half, half), "fsdp", 1)
    output_shard = in_order(core, mine, theirs, 0)

    inner_now = lax.all_gather(expert_inner, "fsdp", axis=1, tiled=True)[0]
    outer_now = lax.all_gather(expert_outer, "fsdp", axis=1, tiled=True)[0]
    extra_width = -(-3 * owners // 128) * 128
    inner_pad = jnp.pad(inner_now, ((0, extra_width), (0, 0)))

    span = 2 * sharers * tokens
    local = jnp.arange(tokens, dtype=jnp.int32)
    positions = jnp.concatenate(
        [
            ((parity ^ a) * sharers + (core ^ c)) * tokens + local
            for a in range(2)
            for c in range(2)
        ]
    )
    token_live = positions[:tokens] < length
    key_live = positions < length
    tables = rotary_tables(positions)
    live_lanes = jnp.broadcast_to(key_live.astype(f32)[:, None], (span, HEAD))
    expert_range = jnp.arange(owners, dtype=jnp.int32)
    hot = expert_ids[:, :, None] == expert_range[None, None, :]
    chosen = jnp.any(hot, axis=1)
    far = jnp.int32(1 << 30)
    order_of = jnp.sum(
        jnp.where(hot, pair_order.reshape(tokens, TOPK)[:, :, None], 0), axis=1
    )
    order_of = jnp.where(chosen & token_live[:, None], order_of, far)
    by_expert = order_of.T
    rank_of = jnp.sum(
        (by_expert[:, None, :] < by_expert[:, :, None]).astype(jnp.int32), axis=-1
    ).T
    rank_of = jnp.where(order_of == far, capacity, jnp.minimum(rank_of, capacity))
    kept = (rank_of < capacity).astype(f32)

    def widened(main, extra):
        pad = -extra.shape[1] % 128
        return jnp.concatenate([main, jnp.pad(extra, ((0, 0), (0, pad)))], axis=1)

    upstream_low = jnp.where(token_live[:, None], cotangent, jnp.zeros((), bf16))
    upstream = upstream_low.astype(f32)
    select = (expert_range[:, None] == (owner ^ jnp.arange(ring))[None, :]).astype(bf16)

    last = PLANES - 1

    def by_plane(*choices):
        out = choices[-1]
        for p in reversed(range(len(choices) - 1)):
            out = jnp.where(plane == p, choices[p], out)
        return out

    def planes_of(block):
        up1 = step_up(block, range(last))
        down1 = step_down(block, range(1, PLANES))
        up2 = step_up(up1, range(1, last))
        down2 = step_down(down1, range(1, last))
        up3 = step_up(up2, [2])
        down3 = step_down(down2, [1])
        return [
            block,
            jnp.where(plane == 0, down1, up1),
            by_plane(down2, down1, down1, up2),
            by_plane(down3, down2, up2, up3),
        ]

    def exchange(rows):
        return [rows[:capacity]] + [
            swap(rows[j * capacity : (j + 1) * capacity], "expert", j) for j in range(1, ring)
        ]

    up_wide = widened(upstream_low, rank_of.astype(bf16))
    pair_order_bits = descending[:-1]
    key_all = gather_plane(key_first, pair_order_bits).reshape(-1, pair_rows + small_tall, quarter)
    value_own = gather_plane(value_first, pair_order_bits)
    key_own = key_all[:, :pair_rows].reshape(width, quarter)
    small_all = key_all[:, pair_rows:].reshape(-1, small_tall * quarter)
    small_all = small_all[:, : 2 * sharers * small_rows * lanes].reshape(devices, -1)
    first_gain = small_all[:, cut[0] : cut[1]].reshape(width).astype(f32)
    second_gain = small_all[:, cut[1] : cut[2]].reshape(width).astype(f32)
    query_scale = small_all[:, cut[2] : cut[3]].reshape(HEAD).astype(f32)
    key_scale = small_all[:, cut[3] : cut[4]].reshape(HEAD).astype(f32)
    router_full = small_all[:, cut[4] : cut[5]].reshape(width, owners)

    output_shard, up_wide, query_first = lax.optimization_barrier(
        (output_shard, up_wide, query_first)
    )
    query_own = gather_plane(query_first, pair_order_bits)
    output_own = gather_plane(gather_planes(output_shard), descending)
    output_peer = swap(output_own, "fsdp", 1)
    d1, d2, d3 = [swap(up_wide, "expert", d * ring) for d in range(1, PLANES)]
    up_planes = [
        up_wide,
        by_plane(d1, d1, d3, d1),
        by_plane(d2, d3, d1, d2),
        by_plane(d3, d2, d2, d3),
    ]
    up_planes, key_late, value_late, query_late = lax.optimization_barrier(
        (up_planes, key_own, value_own, query_own)
    )

    def exchange_all(blocks):
        got = [blocks]
        for j in range(1, ring):
            at = slice(j * capacity, (j + 1) * capacity)
            sent = jnp.concatenate([block[at] for block in blocks], axis=0)
            got.append(swap(sent, "expert", j))
        return [
            [blocks[d][:capacity]]
            + [got[j][d * capacity : (d + 1) * capacity] for j in range(1, ring)]
            for d in range(PLANES)
        ]

    pickers, up_picked = [], []
    for d in range(PLANES):
        rank_rel = matmul(up_planes[d][:, width : width + owners], select)
        hits = rank_rel[:, :, None] == jnp.arange(capacity, dtype=f32)[None, None, :]
        picker = hits.astype(bf16).reshape(tokens, ring * capacity)
        pickers.append(picker)
        up_picked.append(contract_rows(picker, up_planes[d][:, :width], bf16))

    scales = jnp.pad(jnp.stack([query_scale, key_scale]), ((0, 6), (0, 0)))
    hidden_f = hidden_seq.astype(f32)
    first_normed, first_inverse = rms_scale(hidden_f, first_gain)
    first_low = first_normed.astype(bf16)
    key_raw = matmul(first_low, key_own)
    value_low = matmul(first_low, value_own).astype(bf16)
    query_raw = matmul(first_low, query_own)
    key_raw, up_picked = lax.optimization_barrier((key_raw, up_picked))
    up_arrived = exchange_all(up_picked)
    attended, lse = attention_forward(
        query_raw, key_raw, value_low, tables, scales, live_lanes
    )
    left_y = split_columns(first_low, bits - 1)
    far_heads = swap(attended[2 * tokens :], "expert", 1)
    crossed = jnp.concatenate([attended[tokens : 2 * tokens], far_heads[tokens:]], axis=1)
    crossed = swap(crossed, "fsdp", 1)
    attended_full = in_order(
        parity,
        in_order(core, attended[:tokens], crossed[:, :quarter], 1),
        in_order(core, far_heads[:tokens], crossed[:, quarter:], 1),
        1,
    )
    attended_peer = swap(attended_full, "fsdp", 1)
    attended_both = jnp.concatenate([attended_full, attended_peer], axis=0)
    attended_x = split_columns(attended_both, 0)
    branch = in_order(
        core, matmul(attended_full, output_own), matmul(attended_full, output_peer), 1
    )
    residual = hidden_in.astype(f32) + branch
    second_normed, second_inverse = rms_scale(residual, second_gain)
    mixed_in = second_normed.astype(bf16)
    logits = matmul(mixed_in, router_full)
    shown = jnp.where(chosen, logits, masked)
    gate_exp = jnp.where(chosen, jnp.exp(shown - jnp.max(shown, axis=-1, keepdims=True)), 0.0)
    gate_soft = gate_exp / jnp.sum(gate_exp, axis=-1, keepdims=True)

    extra = jnp.concatenate(split_three(gate_soft * kept), axis=1)
    in_planes = planes_of(widened(mixed_in, extra))
    up_arrived, mixed_late = lax.optimization_barrier((up_arrived, mixed_in))
    up_rows = jnp.concatenate([p for parts in up_arrived for p in parts], axis=0)
    picked = [contract_rows(pickers[d], in_planes[d], bf16) for d in range(PLANES)]
    picked[0], up_rows = lax.optimization_barrier((picked[0], up_rows))
    column = jnp.arange(extra_width, dtype=jnp.int32)[None, :]
    own_column = (column % owners == owner) & (column < 3 * owners)
    plane_rows = ring * capacity

    hidden_up = contract_cols(up_rows, outer_now)
    row_inputs, hidden_gated, both_grad, rows_back = [], [], [], []
    for d in range(PLANES):
        rows = exchange(picked[d])
        if d < last:
            rows, picked[d + 1] = lax.optimization_barrier((rows, picked[d + 1]))
        if d == 0:
            rows, left_y, attended_x = lax.optimization_barrier((rows, left_y, attended_x))
        rows = jnp.concatenate(rows, axis=0)
        if d:
            rows, rows_back[-1] = lax.optimization_barrier((rows, rows_back[-1]))
        marks = rows[:, width:].astype(f32)
        row_gate = jnp.sum(jnp.where(own_column, marks, 0.0), axis=1, keepdims=True)
        gate_up = matmul(rows, inner_pad)
        up_back = hidden_up[d * plane_rows : (d + 1) * plane_rows]
        gate_part = gate_up[:, :EFF]
        up_part = gate_up[:, EFF:]
        gate_sigmoid = jax.nn.sigmoid(gate_part)
        activated = gate_part * gate_sigmoid
        hidden_rows = activated * up_part
        gated = (hidden_rows * row_gate).astype(bf16)
        row_gate_grad = jnp.sum(hidden_rows * up_back, axis=1, keepdims=True)
        hidden_grad = up_back * row_gate
        grads = jnp.concatenate(
            [
                hidden_grad * up_part * gate_sigmoid * (1.0 + gate_part * (1.0 - gate_sigmoid)),
                hidden_grad * activated,
            ],
            axis=-1,
        ).astype(bf16)
        part_of = jnp.concatenate(
            [jnp.broadcast_to(p, (p.shape[0], owners)) for p in split_three(row_gate_grad)],
            axis=1,
        )
        part_of = jnp.pad(part_of, ((0, 0), (0, extra_width - 3 * owners)))
        part_of = jnp.where(own_column, part_of, jnp.zeros((), bf16))
        rows_back.append(
            contract_cols(grads, inner_pad, bf16) + jnp.pad(part_of, ((0, 0), (width, 0)))
        )
        row_inputs.append(rows[:, :width])
        hidden_gated.append(gated)
        both_grad.append(grads)
    arrived = [None] * PLANES
    for d in reversed(range(PLANES)):
        block = rows_back[d]
        if d < last:
            block, arrived[d + 1] = lax.optimization_barrier((block, arrived[d + 1]))
        arrived[d] = exchange(block)
    arrived[last], row_inputs, hidden_gated, both_grad = lax.optimization_barrier(
        (arrived[last], row_inputs, hidden_gated, both_grad)
    )
    rows_out = [matmul(gated, outer_now).astype(bf16) for gated in hidden_gated]
    row_inputs = jnp.concatenate(row_inputs, axis=0)
    hidden_gated = jnp.concatenate(hidden_gated, axis=0)
    both_grad = jnp.concatenate(both_grad, axis=0)

    def bring_back(arrived):
        parts = [None] * PLANES
        for d in reversed(range(PLANES)):
            parts[d] = matmul(pickers[d], jnp.concatenate(arrived[d], axis=0))
        near, middle, far_off = parts[1:]
        end = (plane == 0) | (plane == last)
        send = far_off.astype(bf16)
        up = step_up(send, [0]).astype(f32)
        down = step_down(send, [last]).astype(f32)
        send = jnp.where(end, middle, far_off + up + down).astype(bf16)
        up = step_up(send, [0, 1]).astype(f32)
        down = step_down(send, [2, 3]).astype(f32)
        up = step_up(jnp.where(plane == 0, near, middle + up).astype(bf16), [0, 1, 2])
        down = step_down((near + down).astype(bf16), [1, 2, 3])
        return parts[0] + up.astype(f32) + down.astype(f32)

    eff_half = EFF // 2
    inner_sent = contract_rows(pick(row_inputs, (1 - core) * half, half), both_grad, bf16)
    inner_kept = contract_rows(pick(row_inputs, core * half, half), both_grad)
    outer_sent = contract_rows(
        pick(hidden_gated, (1 - core) * eff_half, eff_half), up_rows, bf16
    )
    outer_kept = contract_rows(pick(hidden_gated, core * eff_half, eff_half), up_rows)
    back = bring_back(arrived)
    back, rows_out, inner_sent, inner_kept, outer_sent, outer_kept = lax.optimization_barrier(
        (back, rows_out, inner_sent, inner_kept, outer_sent, outer_kept)
    )
    inner_grad = inner_kept + swap(inner_sent, "fsdp", 1).astype(f32)
    outer_grad = outer_kept + swap(outer_sent, "fsdp", 1).astype(f32)
    out_arrived = exchange_all(rows_out)
    mixed_grad = back[:, :width]
    gate_grad = (
        back[:, width : width + owners]
        + back[:, width + owners : width + 2 * owners]
        + back[:, width + 2 * owners : width + 3 * owners]
    )

    soft_grad = gate_soft * (gate_grad - jnp.sum(gate_soft * gate_grad, axis=-1, keepdims=True))
    logit_grad = soft_grad.astype(bf16)
    router_local = contract_rows(mixed_late, logit_grad)
    mixed_grad = mixed_grad + contract_cols(logit_grad, router_full)
    residual_part, second_terms = rms_back(residual, second_inverse, second_gain, mixed_grad)
    residual_grad = upstream + residual_part
    branch_low = residual_grad.astype(bf16)
    branch_mine = pick(branch_low, core * half, half)
    branch_theirs = pick(branch_low, (1 - core) * half, half)
    attended_grad = (
        contract_cols(branch_mine, output_own) + contract_cols(branch_theirs, output_peer)
    ).astype(bf16)
    far_grad = swap(pick(attended_grad, (1 - parity) * half, half), "expert", 1)
    chip_grad = jnp.stack([pick(attended_grad, parity * half, half), far_grad])
    crossed = swap(pick(chip_grad, (1 - core) * quarter, quarter, 2), "fsdp", 1)
    kept_grad = pick(chip_grad, core * quarter, quarter, 2)
    attended_grad = jnp.concatenate([kept_grad[0], crossed[0], kept_grad[1], crossed[1]], axis=0)

    branch_both = jnp.concatenate([branch_mine, swap(branch_theirs, "fsdp", 1)], axis=0)
    output_sent = contract_rows(attended_x[1], branch_both, bf16)

    attended_grad, output_sent = lax.optimization_barrier((attended_grad, output_sent))
    output_came = swap(output_sent, "expert", 1)
    query_low_grad, key_low_grad, value_low_grad, gain_terms = attention_backward(
        query_raw, key_raw, value_low, attended_grad, lse, tables, scales, live_lanes
    )

    out_arrived, query_low_grad, key_low_grad, value_low_grad = lax.optimization_barrier(
        (out_arrived, query_low_grad, key_low_grad, value_low_grad)
    )
    y_bit = bits - 1
    steps = [key_low_grad, value_low_grad, query_low_grad]
    grads_late = lax.optimization_barrier(
        (steps, [contract_rows(left_y[1], right, bf16) for right in steps])
    )
    steps, sent = grads_late
    key_came = swap(sent[0], "expert", 1 << y_bit)
    output_now = contract_rows(attended_x[0], branch_both) + output_came.astype(f32)
    output_now = scatter_rest(output_now, ascending)
    sent[1], key_came = lax.optimization_barrier((sent[1], key_came))
    value_came = swap(sent[1], "expert", 1 << y_bit)
    sent[2], value_came = lax.optimization_barrier((sent[2], value_came))
    query_came = swap(sent[2], "expert", 1 << y_bit)
    kept = [contract_rows(left_y[0], right) for right in steps]
    blocks = [
        scatter_planes(scatter_rest(k + c.astype(f32), pair_order_bits))
        for k, c in zip(kept, (key_came, value_came, query_came))
    ]
    output_block = scatter_planes(output_now)
    key_late_grad, value_late_grad, query_late_grad = steps
    layer_out = (residual + bring_back(out_arrived)).astype(bf16)

    all_grad = (
        contract_cols(key_late_grad, key_late)
        + contract_cols(value_late_grad, value_late)
        + contract_cols(query_late_grad, query_late)
    )
    own_part, peer_part, far_part, far_peer = jnp.split(all_grad, 4, axis=0)
    crossed = swap(jnp.concatenate([peer_part, far_peer], axis=0).astype(bf16), "fsdp", 1)
    own_part = own_part + crossed[:tokens].astype(f32)
    far_part = (far_part + crossed[tokens:].astype(f32)).astype(bf16)
    far_back = swap(far_part, "expert", 1)
    normed_grad = own_part + far_back.astype(f32)
    hidden_part, first_terms = rms_back(
        hidden_f[:tokens], first_inverse[:tokens], first_gain, normed_grad
    )
    input_grad = residual_grad + hidden_part

    small_grads = jnp.concatenate(
        [
            jnp.sum(first_terms, axis=0).reshape(devices, -1),
            jnp.sum(second_terms, axis=0).reshape(devices, -1),
            jnp.sum(gain_terms[0], axis=0).reshape(devices, -1),
            jnp.sum(gain_terms[1], axis=0).reshape(devices, -1),
            router_local.reshape(devices, -1),
        ],
        axis=1,
    )
    small_grads = jnp.pad(small_grads, ((0, 0), (0, small_rows * lanes - cut[-1])))
    now = small_grads.reshape([PLANES] + [2] * bits + [2, small_rows, lanes])
    at = bits + 1
    sent = lax.dynamic_index_in_dim(now, 1 - core, at, keepdims=False)
    now = lax.dynamic_index_in_dim(now, core, at, keepdims=False) + swap(sent, "fsdp", 1)
    for b in range(bits):
        at = bits - b
        sent = lax.dynamic_index_in_dim(now, 1 - bit_of(b), at, keepdims=False)
        now = lax.dynamic_index_in_dim(now, bit_of(b), at, keepdims=False) + swap(
            sent, "expert", 1 << b
        )
    small_sum = lax.dynamic_index_in_dim(now, plane, 0, keepdims=False)
    for d in range(1, PLANES):
        sent = lax.dynamic_index_in_dim(now, plane ^ d, 0, keepdims=False)
        small_sum = small_sum + swap(sent, "expert", d * ring)
    small_sum = small_sum.reshape(-1)

    def whole_rows(block):
        keep = pick(block, core * rows_dev, rows_dev, 0)
        cross = swap(pick(block, (1 - core) * rows_dev, rows_dev, 0), "fsdp", 1)
        return in_order(core, keep, cross, 1)

    blocks = jnp.stack(blocks).reshape(3, 2, 2, rows_dev, quarter)
    kept = lax.dynamic_index_in_dim(blocks, core, 2, keepdims=False)
    cross = swap(lax.dynamic_index_in_dim(blocks, 1 - core, 2, keepdims=False), "fsdp", 1)
    blocks = in_order(core, kept, cross, 3)
    kept = lax.dynamic_index_in_dim(blocks, parity, 1, keepdims=False)
    cross = lax.dynamic_index_in_dim(blocks, 1 - parity, 1, keepdims=False)
    cross = swap(cross.astype(bf16), "expert", 1).astype(f32)
    key_grad, value_grad, query_grad = in_order(parity, kept, cross, 2)
    weight_grads = [query_grad, key_grad, value_grad, whole_rows(output_block)]
    return (
        layer_out,
        input_grad,
        small_sum[cut[0] : cut[1]],
        weight_grads[0],
        weight_grads[1],
        weight_grads[2],
        small_sum[cut[2] : cut[3]],
        small_sum[cut[3] : cut[4]],
        weight_grads[3],
        small_sum[cut[1] : cut[2]],
        small_sum[cut[4] : cut[5]].reshape(rows_dev, owners),
        inner_grad[None],
        outer_grad[None],
    )


def solution(mesh):
    both = ("expert", "fsdp")
    placed = (
        P(both, None),
        P(both),
        P(both, None),
        P(both, None),
        P(both, None),
        P(both),
        P(both),
        P(both, None),
        P(both),
        P(both, None),
        P("expert", "fsdp", None),
        P("expert", "fsdp", None),
        P(both, None),
        P(both, None),
        P(),
        P(both, None),
    )
    return jax.shard_map(
        on_device,
        mesh=mesh,
        in_specs=placed,
        out_specs=(
            P(both, None),
            P(both, None),
            P(both),
            P(both, None),
            P(both, None),
            P(both, None),
            P(both),
            P(both),
            P(both, None),
            P(both),
            P(both, None),
            P("expert", "fsdp", None),
            P("expert", "fsdp", None),
        ),
        check_vma=False,
    )
```

```python
import math

import jax
import jax.numpy as jnp
from jax import lax
from jax.experimental import pallas as pl
from jax.experimental.pallas import tpu as pltpu
from jax.sharding import PartitionSpec as P

HEAD = 128
EFF = 1024
TOPK = 8
PLANES = 4

epsilon = 1e-06
rope_base = 10000.0
masked = -1e30
bf16 = jnp.bfloat16
f32 = jnp.float32
score_scale = 1.0 / math.sqrt(HEAD)
VMEM_BYTES = 40 * 1024 * 1024


def swap(block, axis, mask):
    count = lax.axis_size(axis)
    return lax.ppermute(block, axis, [(i, i ^ mask) for i in range(count)])


def contract_rows(left, right, out=f32):
    return lax.dot_general(
        left, right, (((0,), (0,)), ((), ())), preferred_element_type=f32
    ).astype(out)


def contract_cols(left, right, out=f32):
    return lax.dot_general(
        left, right, (((1,), (1,)), ((), ())), preferred_element_type=f32
    ).astype(out)


def matmul(left, right):
    return jnp.dot(left, right, preferred_element_type=f32)


def rms_scale(values, gain):
    inverse = lax.rsqrt(jnp.mean(values * values, axis=-1, keepdims=True) + epsilon)
    return (values * inverse * gain, inverse)


def rms_back(values, inverse, gain, upstream):
    scaled = upstream * gain
    inner_sum = jnp.sum(scaled * values, axis=-1, keepdims=True)
    length_now = values.shape[-1]
    grad_values = inverse * scaled - values * (inverse * inverse * inverse) * (
        inner_sum / length_now
    )
    return (grad_values, upstream * values * inverse)


def rotary_tables(positions):
    half_width = HEAD // 2
    freq_steps = jnp.arange(half_width, dtype=f32)
    frequency = jnp.exp(freq_steps * (-2.0 * math.log(rope_base) / HEAD))
    angles = positions.astype(f32)[:, None] * frequency[None, :]
    cosine, sine = jnp.cos(angles), jnp.sin(angles)
    return jnp.stack(
        [
            jnp.concatenate([cosine, cosine], axis=-1),
            jnp.concatenate([-sine, sine], axis=-1),
        ]
    )


def unrope(upstream, cosine, sine):
    return upstream * cosine - pltpu.roll(upstream, HEAD // 2, 1) * sine


def normed_rope(values, gain, cosine, sine):
    normed, inverse = rms_scale(values, gain)
    turned = normed * cosine + pltpu.roll(normed, HEAD // 2, 1) * sine
    return turned.astype(bf16), inverse, normed


def attention_forward(query_raw, key_raw, value_low, tables, scales, live):
    queries, half = query_raw.shape
    span = key_raw.shape[0]
    heads = half // HEAD
    step = min(queries, 256)

    def kernel(q_ref, k_ref, v_ref, table_ref, scale_ref, live_ref, out_ref, lse_ref):
        cosine, sine = table_ref[0], table_ref[1]
        key_low, _, _ = normed_rope(k_ref[...], scale_ref[1:2], cosine, sine)
        value_turned = v_ref[...].astype(f32).T.astype(bf16)
        live_now = jnp.concatenate([live_ref[...]] * (step // HEAD), axis=1) > 0.0
        for part in range(queries // step):
            at = slice(part * step, (part + 1) * step)
            query_low, _, _ = normed_rope(q_ref[at], scale_ref[0:1], cosine[at], sine[at])
            scores = jnp.where(live_now, contract_cols(key_low, query_low), masked)
            peak = jnp.max(scores, axis=0, keepdims=True)
            exponent = jnp.exp((scores - peak) * score_scale)
            running = jnp.sum(exponent, axis=0, keepdims=True)
            turned = matmul(value_turned, exponent.astype(bf16)) / running
            out_ref[at] = turned.T.astype(bf16)
            lse_ref[0, :, at] = jnp.broadcast_to(
                peak * score_scale + jnp.log(running), (8, step)
            )

    column = lambda rows: pl.BlockSpec((rows, HEAD), lambda h: (0, h))
    return pl.pallas_call(
        kernel,
        grid=(heads,),
        in_specs=[
            column(queries),
            column(span),
            column(span),
            pl.BlockSpec((2, span, HEAD), lambda h: (0, 0, 0)),
            pl.BlockSpec((8, HEAD), lambda h: (0, 0)),
            pl.BlockSpec((span, HEAD), lambda h: (0, 0)),
        ],
        out_specs=[column(queries), pl.BlockSpec((1, 8, queries), lambda h: (h, 0, 0))],
        out_shape=[
            jax.ShapeDtypeStruct((queries, half), bf16),
            jax.ShapeDtypeStruct((heads, 8, queries), f32),
        ],
        compiler_params=pltpu.CompilerParams(vmem_limit_bytes=VMEM_BYTES),
        name="attention_forward",
    )(query_raw, key_raw, value_low, tables, scales, live)


def attention_backward(query_raw, key_raw, value_low, attended_grad, lse, tables, scales, live):
    queries, half = query_raw.shape
    span = key_raw.shape[0]
    heads = half // HEAD
    step = min(queries, 256)

    def fold(terms):
        return jnp.sum(terms.reshape(-1, 8, HEAD), axis=0)

    def kernel(
        q_ref, k_ref, v_ref, grad_ref, lse_ref, table_ref, scale_ref, live_ref,
        dq_ref, dk_ref, dv_ref, gains_ref,
    ):
        cosine, sine = table_ref[0], table_ref[1]
        key_raw = k_ref[...]
        key_low, key_inverse, _ = normed_rope(key_raw, scale_ref[1:2], cosine, sine)
        key_turned = key_low.astype(f32).T.astype(bf16)
        live_now = jnp.concatenate([live_ref[...]] * (step // HEAD), axis=1) > 0.0
        key_grad = jnp.zeros((span, HEAD), f32)
        value_grad = jnp.zeros((span, HEAD), f32)
        query_gain = jnp.zeros((8, HEAD), f32)
        for part in range(queries // step):
            at = slice(part * step, (part + 1) * step)
            query_raw = q_ref[at]
            query_low, query_inverse, _ = normed_rope(
                query_raw, scale_ref[0:1], cosine[at], sine[at]
            )
            upstream = grad_ref[at]
            scores = jnp.where(
                live_now, contract_cols(key_low, query_low) * score_scale, masked
            )
            probs = jnp.exp(scores - lse_ref[0, 0:1, at])
            probs_grad = contract_cols(v_ref[...], upstream)
            inner = jnp.sum(probs * probs_grad, axis=0, keepdims=True)
            score_grad = (probs * (probs_grad - inner)).astype(bf16)
            value_grad = value_grad + matmul(probs.astype(bf16), upstream)
            key_grad = key_grad + matmul(score_grad, query_low)
            query_grad = matmul(key_turned, score_grad).T * score_scale
            query_grad, terms = rms_back(
                query_raw,
                query_inverse,
                scale_ref[0:1],
                unrope(query_grad, cosine[at], sine[at]),
            )
            dq_ref[at] = query_grad.astype(bf16)
            query_gain = query_gain + fold(terms)
        dv_ref[...] = value_grad.astype(bf16)
        key_grad, terms = rms_back(
            key_raw, key_inverse, scale_ref[1:2], unrope(key_grad * score_scale, cosine, sine)
        )
        dk_ref[...] = key_grad.astype(bf16)
        gains = jnp.stack([query_gain, fold(terms)])

        @pl.when(pl.program_id(0) == 0)
        def _():
            gains_ref[...] = gains

        @pl.when(pl.program_id(0) > 0)
        def _():
            gains_ref[...] = gains_ref[...] + gains

    column = lambda rows: pl.BlockSpec((rows, HEAD), lambda h: (0, h))
    return pl.pallas_call(
        kernel,
        grid=(heads,),
        in_specs=[
            column(queries),
            column(span),
            column(span),
            column(queries),
            pl.BlockSpec((1, 8, queries), lambda h: (h, 0, 0)),
            pl.BlockSpec((2, span, HEAD), lambda h: (0, 0, 0)),
            pl.BlockSpec((8, HEAD), lambda h: (0, 0)),
            pl.BlockSpec((span, HEAD), lambda h: (0, 0)),
        ],
        out_specs=[
            column(queries),
            column(span),
            column(span),
            pl.BlockSpec((2, 8, HEAD), lambda h: (0, 0, 0)),
        ],
        out_shape=[
            jax.ShapeDtypeStruct((queries, half), bf16),
            jax.ShapeDtypeStruct((span, half), bf16),
            jax.ShapeDtypeStruct((span, half), bf16),
            jax.ShapeDtypeStruct((2, 8, HEAD), f32),
        ],
        compiler_params=pltpu.CompilerParams(vmem_limit_bytes=VMEM_BYTES),
        name="attention_backward",
    )(query_raw, key_raw, value_low, attended_grad, lse, tables, scales, live)


def in_order(flag, first, second, axis):
    return jnp.where(
        flag == 0,
        jnp.concatenate([first, second], axis=axis),
        jnp.concatenate([second, first], axis=axis),
    )


def pick(values, start, width, axis=1):
    return lax.dynamic_slice_in_dim(values, start, width, axis=axis)


def split_three(values):
    high = lax.reduce_precision(values, 8, 7)
    rest = values - high
    middle = lax.reduce_precision(rest, 8, 7)
    low = rest - middle
    return (high.astype(bf16), middle.astype(bf16), low.astype(bf16))


def on_device(
    hidden_in,
    prenorm_gain,
    query_weight,
    key_weight,
    value_weight,
    querynorm_gain,
    keynorm_gain,
    output_weight,
    postnorm_gain,
    router_weight,
    expert_inner,
    expert_outer,
    expert_ids,
    pair_order,
    sequence_lengths,
    cotangent,
):
    tokens, width = hidden_in.shape
    owners = lax.axis_size("expert")
    sharers = lax.axis_size("fsdp")
    devices = owners * sharers
    ring = owners // PLANES
    bits = ring.bit_length() - 1
    capacity = tokens * TOPK // owners
    half = width // 2
    quarter = width // 4
    pair_rows = 2 * width // owners
    owner = lax.axis_index("expert")
    core = lax.axis_index("fsdp")
    parity = owner % 2
    length = lax.dynamic_index_in_dim(sequence_lengths, owner // 2, 0, keepdims=False)

    plane = owner // ring

    def gather_owners(block):
        return lax.all_gather(block, "expert", axis=0, tiled=True)

    def bit_of(b):
        return (owner >> b) & 1

    def gather_planes(block):
        d1, d2, d3 = [swap(block, "expert", d * ring) for d in range(1, PLANES)]
        low, high = plane & 1, plane >> 1
        return in_order(high, in_order(low, block, d1, 0), in_order(low, d2, d3, 0), 0)

    def gather_plane(now, order):
        rows, columns = now.shape[0] // PLANES, now.shape[1]
        now = now.reshape((PLANES,) + (1,) * len(order) + (rows, columns))
        for b in order:
            now = in_order(bit_of(b), now, swap(now, "expert", 1 << b), bits - b)
        return now.reshape(-1, columns)

    def split_columns(values, b):
        each = values.shape[1] // owners

        def side(bit):
            return jnp.concatenate(
                [
                    pick(values, ((k << (b + 1)) + (bit << b)) * each, each << b)
                    for k in range(owners >> (b + 1))
                ],
                axis=1,
            )

        return side(bit_of(b)), side(1 - bit_of(b))

    def scatter_rest(now, order):
        columns = now.shape[1]
        axes = sorted(order[1:], reverse=True)
        for b in order[1:]:
            now = now.reshape([PLANES] + [2] * len(axes) + [-1, columns])
            at = 1 + axes.index(b)
            kept = lax.dynamic_index_in_dim(now, bit_of(b), at, keepdims=False)
            sent = lax.dynamic_index_in_dim(now, 1 - bit_of(b), at, keepdims=False)
            axes.remove(b)
            now = kept + swap(sent.astype(bf16), "expert", 1 << b).astype(f32)
        return now.reshape(PLANES, -1, columns)

    def scatter_planes(now):
        total = lax.dynamic_index_in_dim(now, plane, 0, keepdims=False)
        for d in range(1, PLANES):
            sent = lax.dynamic_index_in_dim(now, plane ^ d, 0, keepdims=False)
            total = total + swap(sent.astype(bf16), "expert", d * ring).astype(f32)
        return total

    descending = list(range(bits))[::-1]
    ascending = list(range(bits))

    def step_up(block, planes):
        return lax.ppermute(
            block, "expert", [(p * ring + i, (p + 1) * ring + i) for p in planes for i in range(ring)]
        )

    def step_down(block, planes):
        return lax.ppermute(
            block, "expert", [(p * ring + i, (p - 1) * ring + i) for p in planes for i in range(ring)]
        )

    rows_dev = width // devices
    small = jnp.concatenate(
        [
            prenorm_gain,
            postnorm_gain,
            querynorm_gain,
            keynorm_gain,
            router_weight.reshape(-1),
        ]
    )
    cut = [0]
    for piece in (prenorm_gain, postnorm_gain, querynorm_gain, keynorm_gain, router_weight):
        cut.append(cut[-1] + piece.size)
    lanes = 128
    small_rows = -(-cut[-1] // (lanes * 16)) * 16
    small = jnp.pad(small, (0, small_rows * lanes - cut[-1])).reshape(small_rows, lanes)
    small_two = in_order(parity, small, swap(small, "expert", 1), 0).reshape(2, 1, -1)
    small_four = in_order(core, small_two, swap(small_two, "fsdp", 1), 1).reshape(-1, quarter)
    small_tall = -(-small_four.shape[0] // 16) * 16
    small_four = jnp.pad(small_four, ((0, small_tall - small_four.shape[0]), (0, 0)))
    other_chip = swap(hidden_in, "expert", 1)
    hidden_own_peer = swap(hidden_in, "fsdp", 1)
    hidden_other_peer = swap(other_chip, "fsdp", 1)
    hidden_seq = jnp.concatenate(
        [hidden_in, hidden_own_peer, other_chip, hidden_other_peer], axis=0
    )

    stacked = jnp.stack([key_weight, value_weight, query_weight])
    mine = pick(stacked, parity * half, half, axis=2)
    theirs = swap(pick(stacked, (1 - parity) * half, half, axis=2), "expert", 1)
    shards = in_order(parity, mine, theirs, 1)
    mine = pick(shards, core * quarter, quarter, axis=2).reshape(3, 2, 1, -1, quarter)
    theirs = swap(pick(shards, (1 - core) * quarter, quarter, axis=2), "fsdp", 1)
    shards = in_order(core, mine, theirs.reshape(mine.shape), 2).reshape(3, pair_rows, quarter)
    key_first = gather_planes(jnp.concatenate([shards[0], small_four], axis=0))
    value_first = gather_planes(shards[1])
    query_first = gather_planes(shards[2])
    mine = pick(output_weight, core * half, half)
    theirs = swap(pick(output_weight, (1 - core) * half, half), "fsdp", 1)
    output_shard = in_order(core, mine, theirs, 0)

    inner_now = lax.all_gather(expert_inner, "fsdp", axis=1, tiled=True)[0]
    outer_now = lax.all_gather(expert_outer, "fsdp", axis=1, tiled=True)[0]
    extra_width = -(-3 * owners // 128) * 128
    inner_pad = jnp.pad(inner_now, ((0, extra_width), (0, 0)))

    span = 2 * sharers * tokens
    local = jnp.arange(tokens, dtype=jnp.int32)
    positions = jnp.concatenate(
        [
            ((parity ^ a) * sharers + (core ^ c)) * tokens + local
            for a in range(2)
            for c in range(2)
        ]
    )
    token_live = positions[:tokens] < length
    key_live = positions < length
    tables = rotary_tables(positions)
    live_lanes = jnp.broadcast_to(key_live.astype(f32)[:, None], (span, HEAD))
    expert_range = jnp.arange(owners, dtype=jnp.int32)
    hot = expert_ids[:, :, None] == expert_range[None, None, :]
    chosen = jnp.any(hot, axis=1)
    far = jnp.int32(1 << 30)
    order_of = jnp.sum(
        jnp.where(hot, pair_order.reshape(tokens, TOPK)[:, :, None], 0), axis=1
    )
    order_of = jnp.where(chosen & token_live[:, None], order_of, far)
    by_expert = order_of.T
    rank_of = jnp.sum(
        (by_expert[:, None, :] < by_expert[:, :, None]).astype(jnp.int32), axis=-1
    ).T
    rank_of = jnp.where(order_of == far, capacity, jnp.minimum(rank_of, capacity))
    kept = (rank_of < capacity).astype(f32)

    def widened(main, extra):
        pad = -extra.shape[1] % 128
        return jnp.concatenate([main, jnp.pad(extra, ((0, 0), (0, pad)))], axis=1)

    upstream_low = jnp.where(token_live[:, None], cotangent, jnp.zeros((), bf16))
    upstream = upstream_low.astype(f32)
    select = (expert_range[:, None] == (owner ^ jnp.arange(ring))[None, :]).astype(bf16)

    last = PLANES - 1

    def by_plane(*choices):
        out = choices[-1]
        for p in reversed(range(len(choices) - 1)):
            out = jnp.where(plane == p, choices[p], out)
        return out

    def planes_of(block):
        up1 = step_up(block, range(last))
        down1 = step_down(block, range(1, PLANES))
        up2 = step_up(up1, range(1, last))
        down2 = step_down(down1, range(1, last))
        up3 = step_up(up2, [2])
        down3 = step_down(down2, [1])
        return [
            block,
            jnp.where(plane == 0, down1, up1),
            by_plane(down2, down1, down1, up2),
            by_plane(down3, down2, up2, up3),
        ]

    def exchange(rows):
        return [rows[:capacity]] + [
            swap(rows[j * capacity : (j + 1) * capacity], "expert", j) for j in range(1, ring)
        ]

    up_wide = widened(upstream_low, rank_of.astype(bf16))
    pair_order_bits = descending[:-1]
    key_all = gather_plane(key_first, pair_order_bits).reshape(-1, pair_rows + small_tall, quarter)
    value_own = gather_plane(value_first, pair_order_bits)
    key_own = key_all[:, :pair_rows].reshape(width, quarter)
    small_all = key_all[:, pair_rows:].reshape(-1, small_tall * quarter)
    small_all = small_all[:, : 2 * sharers * small_rows * lanes].reshape(devices, -1)
    first_gain = small_all[:, cut[0] : cut[1]].reshape(width).astype(f32)
    second_gain = small_all[:, cut[1] : cut[2]].reshape(width).astype(f32)
    query_scale = small_all[:, cut[2] : cut[3]].reshape(HEAD).astype(f32)
    key_scale = small_all[:, cut[3] : cut[4]].reshape(HEAD).astype(f32)
    router_full = small_all[:, cut[4] : cut[5]].reshape(width, owners)

    output_shard, up_wide, query_first = lax.optimization_barrier(
        (output_shard, up_wide, query_first)
    )
    query_own = gather_plane(query_first, pair_order_bits)
    output_own = gather_plane(gather_planes(output_shard), descending)
    output_peer = swap(output_own, "fsdp", 1)
    d1, d2, d3 = [swap(up_wide, "expert", d * ring) for d in range(1, PLANES)]
    up_planes = [
        up_wide,
        by_plane(d1, d1, d3, d1),
        by_plane(d2, d3, d1, d2),
        by_plane(d3, d2, d2, d3),
    ]
    up_planes, key_late, value_late, query_late = lax.optimization_barrier(
        (up_planes, key_own, value_own, query_own)
    )

    def exchange_all(blocks):
        got = [blocks]
        for j in range(1, ring):
            at = slice(j * capacity, (j + 1) * capacity)
            sent = jnp.concatenate([block[at] for block in blocks], axis=0)
            got.append(swap(sent, "expert", j))
        return [
            [blocks[d][:capacity]]
            + [got[j][d * capacity : (d + 1) * capacity] for j in range(1, ring)]
            for d in range(len(blocks))
        ]

    pickers, up_picked = [], []
    for d in range(PLANES):
        rank_rel = matmul(up_planes[d][:, width : width + owners], select)
        hits = rank_rel[:, :, None] == jnp.arange(capacity, dtype=f32)[None, None, :]
        picker = hits.astype(bf16).reshape(tokens, ring * capacity)
        pickers.append(picker)
        up_picked.append(contract_rows(picker, up_planes[d][:, :width], bf16))

    scales = jnp.pad(jnp.stack([query_scale, key_scale]), ((0, 6), (0, 0)))
    hidden_f = hidden_seq.astype(f32)
    first_normed, first_inverse = rms_scale(hidden_f, first_gain)
    first_low = first_normed.astype(bf16)
    key_raw = matmul(first_low, key_own)
    value_low = matmul(first_low, value_own).astype(bf16)
    query_raw = matmul(first_low, query_own)
    key_raw, up_picked = lax.optimization_barrier((key_raw, up_picked))
    up_arrived = exchange_all(up_picked)
    attended, lse = attention_forward(
        query_raw, key_raw, value_low, tables, scales, live_lanes
    )
    left_y = split_columns(first_low, bits - 1)
    attended, up_arrived = lax.optimization_barrier((attended, up_arrived))
    far_heads = swap(attended[2 * tokens :], "expert", 1)
    crossed = jnp.concatenate([attended[tokens : 2 * tokens], far_heads[tokens:]], axis=1)
    crossed = swap(crossed, "fsdp", 1)
    attended_full = in_order(
        parity,
        in_order(core, attended[:tokens], crossed[:, :quarter], 1),
        in_order(core, far_heads[:tokens], crossed[:, quarter:], 1),
        1,
    )
    attended_peer = swap(attended_full, "fsdp", 1)
    attended_both = jnp.concatenate([attended_full, attended_peer], axis=0)
    attended_x = split_columns(attended_both, 0)
    branch = in_order(
        core, matmul(attended_full, output_own), matmul(attended_full, output_peer), 1
    )
    residual = hidden_in.astype(f32) + branch
    second_normed, second_inverse = rms_scale(residual, second_gain)
    mixed_in = second_normed.astype(bf16)
    logits = matmul(mixed_in, router_full)
    shown = jnp.where(chosen, logits, masked)
    gate_exp = jnp.where(chosen, jnp.exp(shown - jnp.max(shown, axis=-1, keepdims=True)), 0.0)
    gate_soft = gate_exp / jnp.sum(gate_exp, axis=-1, keepdims=True)

    extra = jnp.concatenate(split_three(gate_soft * kept), axis=1)
    in_planes = planes_of(widened(mixed_in, extra))
    up_rows = jnp.concatenate([p for parts in up_arrived for p in parts], axis=0)
    picked = [contract_rows(pickers[d], in_planes[d], bf16) for d in range(PLANES)]
    picked[0], up_rows = lax.optimization_barrier((picked[0], up_rows))
    column = jnp.arange(extra_width, dtype=jnp.int32)[None, :]
    own_column = (column % owners == owner) & (column < 3 * owners)
    plane_rows = ring * capacity

    hidden_up = contract_cols(up_rows, outer_now)
    row_inputs, hidden_gated, both_grad, rows_back = [], [], [], []
    for d in range(PLANES):
        rows = exchange(picked[d])
        if d < last:
            rows, picked[d + 1] = lax.optimization_barrier((rows, picked[d + 1]))
        if d == 0:
            rows, left_y, attended_x = lax.optimization_barrier((rows, left_y, attended_x))
        rows = jnp.concatenate(rows, axis=0)
        if d:
            rows, rows_back[-1] = lax.optimization_barrier((rows, rows_back[-1]))
        marks = rows[:, width:].astype(f32)
        row_gate = jnp.sum(jnp.where(own_column, marks, 0.0), axis=1, keepdims=True)
        gate_up = matmul(rows, inner_pad)
        up_back = hidden_up[d * plane_rows : (d + 1) * plane_rows]
        gate_part = gate_up[:, :EFF]
        up_part = gate_up[:, EFF:]
        gate_sigmoid = jax.nn.sigmoid(gate_part)
        activated = gate_part * gate_sigmoid
        hidden_rows = activated * up_part
        gated = (hidden_rows * row_gate).astype(bf16)
        row_gate_grad = jnp.sum(hidden_rows * up_back, axis=1, keepdims=True)
        hidden_grad = up_back * row_gate
        grads = jnp.concatenate(
            [
                hidden_grad * up_part * gate_sigmoid * (1.0 + gate_part * (1.0 - gate_sigmoid)),
                hidden_grad * activated,
            ],
            axis=-1,
        ).astype(bf16)
        part_of = jnp.concatenate(
            [jnp.broadcast_to(p, (p.shape[0], owners)) for p in split_three(row_gate_grad)],
            axis=1,
        )
        part_of = jnp.pad(part_of, ((0, 0), (0, extra_width - 3 * owners)))
        part_of = jnp.where(own_column, part_of, jnp.zeros((), bf16))
        rows_back.append(
            contract_cols(grads, inner_pad, bf16) + jnp.pad(part_of, ((0, 0), (width, 0)))
        )
        row_inputs.append(rows[:, :width])
        hidden_gated.append(gated)
        both_grad.append(grads)
    arrived = [None] * PLANES
    for d in reversed(range(PLANES)):
        block = rows_back[d]
        if d < last:
            block, arrived[d + 1] = lax.optimization_barrier((block, arrived[d + 1]))
        arrived[d] = exchange(block)
    arrived[3], row_inputs, both_grad = lax.optimization_barrier(
        (arrived[3], row_inputs, both_grad)
    )
    row_inputs = jnp.concatenate(row_inputs, axis=0)
    both_grad = jnp.concatenate(both_grad, axis=0)
    inner_local = contract_rows(row_inputs, both_grad, bf16)
    arrived[2], gated_rows = lax.optimization_barrier((arrived[2], hidden_gated))
    outer_local = contract_rows(jnp.concatenate(gated_rows, axis=0), up_rows, bf16)
    arrived[1], late_gated = lax.optimization_barrier((arrived[1], gated_rows))
    rows_out = [matmul(gated, outer_now).astype(bf16) for gated in late_gated]

    def relayed(arrived):
        parts = [None] * PLANES
        for d in reversed(range(PLANES)):
            parts[d] = matmul(pickers[d], jnp.concatenate(arrived[d], axis=0))
        near, middle, far_off = parts[1:]
        end = (plane == 0) | (plane == last)
        send = far_off.astype(bf16)
        up = step_up(send, [0]).astype(f32)
        down = step_down(send, [last]).astype(f32)
        send = jnp.where(end, middle, far_off + up + down).astype(bf16)
        up = step_up(send, [0, 1]).astype(f32)
        down = step_down(send, [2, 3]).astype(f32)
        up = step_up(jnp.where(plane == 0, near, middle + up).astype(bf16), [0, 1, 2])
        down = step_down((near + down).astype(bf16), [1, 2, 3])
        return parts[0] + up.astype(f32) + down.astype(f32)

    back = relayed(arrived)
    back, rows_out, inner_local, outer_local = lax.optimization_barrier(
        (back, rows_out, inner_local, outer_local)
    )
    inner_grad = lax.psum_scatter(
        inner_local, "fsdp", scatter_dimension=0, tiled=True
    ).astype(f32)
    outer_grad = lax.psum_scatter(
        outer_local, "fsdp", scatter_dimension=0, tiled=True
    ).astype(f32)
    mixed_grad = back[:, :width]
    gate_grad = (
        back[:, width : width + owners]
        + back[:, width + owners : width + 2 * owners]
        + back[:, width + 2 * owners : width + 3 * owners]
    )

    soft_grad = gate_soft * (gate_grad - jnp.sum(gate_soft * gate_grad, axis=-1, keepdims=True))
    logit_grad = soft_grad.astype(bf16)
    router_local = contract_rows(mixed_in, logit_grad)
    mixed_grad = mixed_grad + contract_cols(logit_grad, router_full)
    residual_part, second_terms = rms_back(residual, second_inverse, second_gain, mixed_grad)
    residual_grad = upstream + residual_part
    branch_low = residual_grad.astype(bf16)
    branch_mine = pick(branch_low, core * half, half)
    branch_theirs = pick(branch_low, (1 - core) * half, half)
    attended_grad = (
        contract_cols(branch_mine, output_own) + contract_cols(branch_theirs, output_peer)
    ).astype(bf16)
    far_grad = swap(pick(attended_grad, (1 - parity) * half, half), "expert", 1)
    rows_out, far_grad = lax.optimization_barrier((rows_out, far_grad))
    out_arrived = exchange_all(rows_out)
    chip_grad = jnp.stack([pick(attended_grad, parity * half, half), far_grad])
    crossed = swap(pick(chip_grad, (1 - core) * quarter, quarter, 2), "fsdp", 1)
    kept_grad = pick(chip_grad, core * quarter, quarter, 2)
    attended_grad = jnp.concatenate([kept_grad[0], crossed[0], kept_grad[1], crossed[1]], axis=0)

    branch_both = jnp.concatenate([branch_mine, swap(branch_theirs, "fsdp", 1)], axis=0)
    output_sent = contract_rows(attended_x[1], branch_both, bf16)

    attended_grad, output_sent = lax.optimization_barrier((attended_grad, output_sent))
    output_came = swap(output_sent, "expert", 1)
    query_low_grad, key_low_grad, value_low_grad, gain_terms = attention_backward(
        query_raw, key_raw, value_low, attended_grad, lse, tables, scales, live_lanes
    )

    y_bit = bits - 1
    steps = jnp.concatenate([key_low_grad, value_low_grad, query_low_grad], axis=1)
    sent = contract_rows(left_y[1], steps, bf16)
    sent, steps = lax.optimization_barrier((sent, steps))
    weights_came = swap(sent, "expert", 1 << y_bit)
    all_grad = sum(
        contract_cols(steps[:, i * quarter : (i + 1) * quarter], weight)
        for i, weight in enumerate((key_own, value_own, query_own))
    )
    own_part, peer_part, far_part, far_peer = jnp.split(all_grad, 4, axis=0)
    crossed = swap(jnp.concatenate([peer_part, far_peer], axis=0).astype(bf16), "fsdp", 1)
    own_part = own_part + crossed[:tokens].astype(f32)
    far_part = (far_part + crossed[tokens:].astype(f32)).astype(bf16)
    far_back = swap(far_part, "expert", 1)
    weights_came, output_came = lax.optimization_barrier((weights_came, output_came))
    output_now = contract_rows(attended_x[0], branch_both) + output_came.astype(f32)
    output_now = scatter_rest(output_now, ascending)
    weights_now = contract_rows(left_y[0], steps) + weights_came.astype(f32)
    weights_now = scatter_rest(weights_now, pair_order_bits)
    output_now, far_back, inner_grad, outer_grad = lax.optimization_barrier(
        (output_now, far_back, inner_grad, outer_grad)
    )
    blocks = scatter_planes(weights_now)
    output_block = scatter_planes(output_now)
    mixed = relayed(out_arrived)
    blocks, mixed = lax.optimization_barrier((blocks, mixed))
    layer_out = residual + mixed
    layer_out = layer_out.astype(bf16)

    normed_grad = own_part + far_back.astype(f32)
    hidden_part, first_terms = rms_back(
        hidden_f[:tokens], first_inverse[:tokens], first_gain, normed_grad
    )
    input_grad = residual_grad + hidden_part

    small_grads = jnp.concatenate(
        [
            jnp.sum(first_terms, axis=0).reshape(devices, -1),
            jnp.sum(second_terms, axis=0).reshape(devices, -1),
            jnp.sum(gain_terms[0], axis=0).reshape(devices, -1),
            jnp.sum(gain_terms[1], axis=0).reshape(devices, -1),
            router_local.reshape(devices, -1),
        ],
        axis=1,
    )
    small_grads = jnp.pad(small_grads, ((0, 0), (0, small_rows * lanes - cut[-1])))
    now = small_grads.reshape([PLANES] + [2] * bits + [2, small_rows, lanes])
    at = bits + 1
    sent = lax.dynamic_index_in_dim(now, 1 - core, at, keepdims=False)
    now = lax.dynamic_index_in_dim(now, core, at, keepdims=False) + swap(sent, "fsdp", 1)
    for b in range(bits):
        at = bits - b
        sent = lax.dynamic_index_in_dim(now, 1 - bit_of(b), at, keepdims=False)
        now = lax.dynamic_index_in_dim(now, bit_of(b), at, keepdims=False) + swap(
            sent, "expert", 1 << b
        )
    small_sum = lax.dynamic_index_in_dim(now, plane, 0, keepdims=False)
    for d in range(1, PLANES):
        sent = lax.dynamic_index_in_dim(now, plane ^ d, 0, keepdims=False)
        small_sum = small_sum + swap(sent, "expert", d * ring)
    small_sum = small_sum.reshape(-1)

    def whole_rows(block):
        keep = pick(block, core * rows_dev, rows_dev, 0)
        cross = swap(pick(block, (1 - core) * rows_dev, rows_dev, 0), "fsdp", 1)
        return in_order(core, keep, cross, 1)

    blocks = blocks.reshape(2, 2, rows_dev, 3, quarter).transpose(3, 0, 1, 2, 4)
    kept = lax.dynamic_index_in_dim(blocks, core, 2, keepdims=False)
    cross = swap(lax.dynamic_index_in_dim(blocks, 1 - core, 2, keepdims=False), "fsdp", 1)
    blocks = in_order(core, kept, cross, 3)
    kept = lax.dynamic_index_in_dim(blocks, parity, 1, keepdims=False)
    cross = lax.dynamic_index_in_dim(blocks, 1 - parity, 1, keepdims=False)
    cross = swap(cross.astype(bf16), "expert", 1).astype(f32)
    key_grad, value_grad, query_grad = in_order(parity, kept, cross, 2)
    weight_grads = [query_grad, key_grad, value_grad, whole_rows(output_block)]
    return (
        layer_out,
        input_grad,
        small_sum[cut[0] : cut[1]],
        weight_grads[0],
        weight_grads[1],
        weight_grads[2],
        small_sum[cut[2] : cut[3]],
        small_sum[cut[3] : cut[4]],
        weight_grads[3],
        small_sum[cut[1] : cut[2]],
        small_sum[cut[4] : cut[5]].reshape(rows_dev, owners),
        inner_grad[None],
        outer_grad[None],
    )


def solution(mesh):
    both = ("expert", "fsdp")
    placed = (
        P(both, None),
        P(both),
        P(both, None),
        P(both, None),
        P(both, None),
        P(both),
        P(both),
        P(both, None),
        P(both),
        P(both, None),
        P("expert", "fsdp", None),
        P("expert", "fsdp", None),
        P(both, None),
        P(both, None),
        P(),
        P(both, None),
    )
    return jax.shard_map(
        on_device,
        mesh=mesh,
        in_specs=placed,
        out_specs=(
            P(both, None),
            P(both, None),
            P(both),
            P(both, None),
            P(both, None),
            P(both, None),
            P(both),
            P(both),
            P(both, None),
            P(both),
            P(both, None),
            P("expert", "fsdp", None),
            P("expert", "fsdp", None),
        ),
        check_vma=False,
    )
```
